128 devices in a mesh: gx: 4 (over y_hi, core), gy: 32 (over y_lo, z, x).
Axes of the slice: x: 4, y: 4 (y_hi: 2, y_lo: 2; y = y_hi * 2 + y_lo), z: 4, core: 2. Of those that a mesh axis runs over, the one named last changes fastest.
Arguments:
- tokens: bfloat16 [256, 18432], P(None, ('gx', 'gy')), may hold values from -64 to 64
- ln_gain: float32 [18432], P('gx'), may hold values from 0.25 to 1.75
- w_query: bfloat16 [18432, 12288], P('gx', 'gy'), may hold values from -0.046875 to 0.046875
- w_entries: bfloat16 [18432, 512], P(('gx', 'gy')), may hold values from -0.09375 to 0.09375
- w_out: bfloat16 [12288, 18432], P('gy', 'gx'), may hold values from -0.0546875 to 0.0546875
- w_gate: bfloat16 [18432, 18432], P('gx', 'gy'), may hold values from -0.046875 to 0.046875
- w_up: bfloat16 [18432, 18432], P('gx', 'gy'), may hold values from -0.046875 to 0.046875
- w_down: bfloat16 [18432, 18432], P('gy', 'gx'), may hold values from -0.046875 to 0.046875
- cache_keys: bfloat16 [256, 1024, 256], P(('gx', 'gy')), may hold values from -512 to 512
- cache_values: bfloat16 [256, 1024, 256], P(('gx', 'gy')), may hold values from -6 to 6
- lengths: int32 [256], replicated, may hold values from 2 to 1024, as said below
Outputs:
- layer_out: float32 [256, 18432], P(None, ('gx', 'gy'))
The draws below stay inside these ranges and needn't reach their ends.
Inputs may be any that keep to these rules, and one draw needn't show every extreme that they name: `lengths`: some row uses all 1024 positions.
All inputs are finite; a program needn't handle non-finite values.
Results may differ from the reference program's by a relative error of at most 0.0025.
Values may be sent and summed in bfloat16 or wider, within the bound.
A program may use at most 128 MiB of HBM per device.

```python
import math
import jax
import jax.numpy as jnp
from jax import lax

D = 18432
H = 48
DH = 256
FF = 18432
CTX = 1024
BATCH = 256


def draw_tokens(key, part):
    key = jax.random.fold_in(key, 11)
    key_base, key_cols, key_rows = jax.random.split(key, 3)
    ramp = jnp.exp(math.log(3.0) * jnp.arange(D, dtype=jnp.float32) / D)
    columns = jnp.exp(jax.random.uniform(key_cols, (D,), minval=0.0, maxval=math.log(10.0))) * ramp
    row_scale = jnp.exp(jax.random.uniform(key_rows, (BATCH, 1), minval=0.0, maxval=math.log(10.0)))
    base = jax.random.truncated_normal(key_base, -4.0, 4.0, (BATCH, D))
    return (0.05 * base * row_scale * columns[None, :]).astype(jnp.bfloat16)


def draw_cache_keys(key, part):
    key = jax.random.fold_in(key, 23)
    key_base = jax.random.fold_in(key, 0)
    keys = jax.random.truncated_normal(key_base, -4.0, 4.0, (BATCH, CTX, DH))
    return keys.astype(jnp.bfloat16)


def draw_lengths(key, part):
    key = jax.random.fold_in(key, 37)
    key_lens, key_where = jax.random.split(key, 2)
    drawn = jax.random.randint(key_lens, (BATCH,), 2, CTX + 1)
    chosen = jax.random.randint(key_where, (), 0, BATCH)
    return jnp.where(jnp.arange(BATCH, dtype=jnp.int32) == chosen, CTX, drawn).astype(jnp.int32)


def levels(own_key, shape, cuts, least, top_value):
    loudness = 1.0
    for axis_at, parts in cuts:
        heights = jax.random.uniform(jax.random.fold_in(jax.random.fold_in(own_key, 6), axis_at), (parts,), jnp.float32, least / len(cuts), top_value / len(cuts))
        loudness = loudness * jnp.repeat(jnp.exp(heights), shape[axis_at] // parts).reshape((-1,) + (1,) * (len(shape) - 1 - axis_at))
    return loudness


def centred(stream_key, extent, deviation, limit, shards=(), kind=jnp.bfloat16):
    level = levels(stream_key, extent, shards, -0.22, 0.18) if shards else 1.0
    values = jax.random.normal(stream_key, extent, jnp.float32) * deviation * level
    return jnp.minimum(jnp.maximum(values, -limit), limit).astype(kind)


def setup_inputs(seed: int = 0) -> dict:
    splits = jax.random.split(jax.random.key(seed), 12)
    return {
        "tokens": draw_tokens(jax.random.fold_in(splits[11], 71), 0),
        "ln_gain": jnp.clip(1.0 + 0.15 * jax.random.normal(splits[1], (D,), jnp.float32), 0.25, 1.75),
        "w_query": centred(splits[2], (D, H * DH), D ** -0.5, 0.046875, ((0, 4), (1, 32))),
        "w_entries": centred(splits[3], (D, 2 * DH), (D // 4) ** -0.5, 0.09375, ((0, 128),)),
        "w_out": centred(splits[4], (H * DH, D), (H * DH) ** -0.5, 0.0546875, ((0, 32), (1, 4))),
        "w_gate": centred(splits[5], (D, FF), D ** -0.5, 0.046875, ((0, 4), (1, 32))),
        "w_up": centred(splits[6], (D, FF), D ** -0.5, 0.046875, ((0, 4), (1, 32))),
        "w_down": centred(splits[7], (FF, D), FF ** -0.5, 0.046875, ((0, 32), (1, 4))),
        "cache_keys": draw_cache_keys(jax.random.fold_in(splits[11], 71), 0),
        "cache_values": centred(splits[9], (BATCH, CTX, DH), 1.0, 6.0, ((0, 128),)),
        "lengths": draw_lengths(jax.random.fold_in(splits[11], 71), 0),
    }


EPS = 1e-05

def rotate(values, positions, offset, head_size):
    rows, width = values.shape
    even_columns = offset + 2 * jnp.arange(width // 2, dtype=jnp.int32)
    pair_index = (even_columns % head_size // 2).astype(jnp.float32)
    frequency = jnp.exp(pair_index * (-2.0 * math.log(10000.0) / head_size))
    angle = positions.astype(jnp.float32)[:, None] * frequency[None, :]
    cosine = jnp.cos(angle)
    sine = jnp.sin(angle)
    pairs = values.reshape(rows, width // 2, 2)
    first = pairs[:, :, 0]
    second = pairs[:, :, 1]
    turned = jnp.stack([first * cosine - second * sine, first * sine + second * cosine], axis=2)
    return turned.reshape(rows, width)

def reference(tokens, ln_gain, w_query, w_entries, w_out, w_gate, w_up, w_down, cache_keys, cache_values, lengths):
    values32 = tokens.astype(jnp.float32)
    average = lax.optimization_barrier(jnp.sum(values32, axis=1)) / D
    squares = lax.optimization_barrier(jnp.sum(values32 * values32, axis=1)) / D
    factor = lax.rsqrt(squares - average * average + EPS)
    normed = ((values32 - average[:, None]) * factor[:, None] * ln_gain[None, :]).astype(jnp.bfloat16)
    query = rotate(jnp.dot(normed, w_query, preferred_element_type=jnp.float32), lengths, 0, DH).astype(jnp.bfloat16)
    entries = jnp.dot(normed, w_entries, preferred_element_type=jnp.float32)
    new_key = rotate(entries[:, :DH], lengths, 0, DH).astype(jnp.bfloat16)
    new_value = entries[:, DH:].astype(jnp.bfloat16)
    gate = jnp.dot(normed, w_gate, preferred_element_type=jnp.float32)
    upward = jnp.dot(normed, w_up, preferred_element_type=jnp.float32)
    hidden = (jax.nn.silu(gate) * upward).astype(jnp.bfloat16)
    scale = 1.0 / math.sqrt(DH)
    positions = jnp.arange(CTX, dtype=jnp.int32)

    def attend(operands):
        query_row, keys, values, key_row, value_row, length = operands
        heads_query = query_row.reshape(H, DH)
        scores = jnp.dot(heads_query, keys.T, preferred_element_type=jnp.float32) * scale
        scores = jnp.where(positions[None, :] < length, scores, -1e+30)
        own = jnp.dot(heads_query, key_row, preferred_element_type=jnp.float32) * scale
        peak = jnp.maximum(lax.optimization_barrier(jnp.max(scores, axis=1)), own)
        expd = jnp.exp(scores - peak[:, None])
        own_exp = jnp.exp(own - peak)
        denom = lax.optimization_barrier(jnp.sum(expd, axis=1)) + own_exp
        weights = (expd / denom[:, None]).astype(jnp.bfloat16)
        own_weight = (own_exp / denom).astype(jnp.bfloat16)
        mixed = jnp.dot(weights, values, preferred_element_type=jnp.float32)
        mixed = mixed + own_weight.astype(jnp.float32)[:, None] * value_row.astype(jnp.float32)[None, :]
        return mixed.astype(jnp.bfloat16).reshape(H * DH)
    attention = lax.map(attend, (query, cache_keys, cache_values, new_key, new_value, lengths))
    projected = jnp.dot(attention, w_out, preferred_element_type=jnp.float32)
    projected = projected + jnp.dot(hidden, w_down, preferred_element_type=jnp.float32)
    return values32 + projected
```

```python
import math

import jax
import jax.numpy as jnp
from jax import lax
from jax.experimental import pallas as pl
from jax.experimental.pallas import tpu as pltpu
from jax.sharding import PartitionSpec as P

D = 18432
H = 48
DH = 256
CTX = 1024
EPS = 1e-05
ROWS = 256
COLS = 144
PA, PB = 80, 64
QC = 384
EC = 512
FC = 576
SLAB = 4608
WIDE = 1152
BF = jnp.bfloat16
F32 = jnp.float32
LOG_BASE = -2.0 * math.log(10000.0) / DH


def dot(a, b):
    return jnp.dot(a, b, preferred_element_type=F32)


def remote(src, dst, send, recv, gx, gy):
    return pltpu.make_async_remote_copy(
        src_ref=src,
        dst_ref=dst,
        send_sem=send,
        recv_sem=recv,
        device_id={"gx": gx, "gy": gy},
        device_id_type=pl.DeviceIdType.MESH,
    )


def place(y, z, x):
    return y * 16 + z * 4 + x


def swap_pairs(v):
    width = v.shape[1]
    even = lax.rem(lax.broadcasted_iota(jnp.int32, v.shape, 1), 2) == 0
    return jnp.where(even, pltpu.roll(v, width - 1, 1), pltpu.roll(v, 1, 1))


def rope_tables(positions, offset, shape):
    col = lax.broadcasted_iota(jnp.int32, shape, 1)
    even = lax.rem(col, 2) == 0
    pair = lax.rem(col + offset, DH) // 2
    angle = positions * jnp.exp(pair.astype(F32) * LOG_BASE)
    sine = jnp.sin(angle)
    return jnp.cos(angle), jnp.where(even, -sine, sine)


SCRATCH = dict(
    wq0=((4, 2, 4, PA, QC), BF),
    wq1=((4, 2, 4, PB, QC), BF),
    wg0=((4, 2, 4, PA, FC), BF),
    wg1=((4, 2, 4, PB, FC), BF),
    wu0=((4, 2, 4, PA, FC), BF),
    wu1=((4, 2, 4, PB, FC), BF),
    wev=((COLS, EC), BF),
    wov=((QC, SLAB), BF),
    wdv=((FC, SLAB), BF),
    keys=((2, CTX, DH), BF),
    vals=((2, CTX, DH), BF),
    pad=((ROWS, ROWS), F32),
    gpad=((128, 128), F32),
    gcol=((SLAB, 128), F32),
    xt0=((4, 2, 4, PA, ROWS), BF),
    xt1=((4, 2, 4, PB, ROWS), BF),
    st=((8, 128), F32),
    str_=((3, 8, 128), F32),
    st2=((8, 128), F32),
    st2r=((32, 8, 128), F32),
    stat=((8, ROWS), F32),
    nrm0=((8 * PA, ROWS), BF),
    nrm1=((8 * PB, ROWS), BF),
    pq=((ROWS, QC), F32),
    pe=((ROWS, EC), F32),
    pg=((ROWS, FC), F32),
    pu=((ROWS, FC), F32),
    sq1=((2, 64, QC + EC), BF),
    rq1=((2, 64, QC + EC), BF),
    sq2=((64, QC + EC), BF),
    rq2=((64, QC + EC), BF),
    sg1=((2, 2, 64, FC), BF),
    rg1=((2, 2, 64, FC), BF),
    sg2=((2, 64, FC), BF),
    rg2=((2, 64, FC), BF),
    lenb=((64, QC), F32),
    cosq=((64, QC), F32),
    sinq=((64, QC), F32),
    qf=((3, 64, 128), F32),
    ef=((4, 64, 128), F32),
    msg=((512, 128), F32),
    mq=((32, 16, 128), BF),
    mr=((32, 16, 128), BF),
    pieces=((96, 128), F32),
    aback=((32, 8, 128), F32),
    abackr=((32, 8, 128), F32),
    att64=((3, 64, 128), F32),
    attall=((4, 64, QC), BF),
    hidall=((4, 64, FC), BF),
    outp=((ROWS, SLAB), F32),
    eT=((2, 4, 4, COLS, ROWS), BF),
    r0=((3, 2, 4, PA, ROWS), BF),
    r1=((3, 2, 4, PB, ROWS), BF),
    s0=((2, 4, PA, ROWS), BF),
    s1=((2, 4, PB, ROWS), BF),
    r0b=((8, PA, ROWS), BF),
    r1b=((8, PB, ROWS), BF),
)
SEMS = dict(
    lw=(2, 4, 3),
    lx=(5,),
    stg=(2, 3),
    sts=(2,),
    a0=(2, 8),
    a1=(2, 8),
    b0=(2, 4),
    b1=(2, 4),
    cq=(2, 2),
    cg=(2, 2),
    mqs=(2,),
    abs_=(2,),
    ga=(2, 3),
    gh=(2, 3),
    e0=(2, 3),
    e1=(2, 3),
    f0=(2, 8),
    f1=(2, 8),
)
NAMES = list(SCRATCH) + list(SEMS)


class Refs:
    pass


def kernel(tok, gain, lens, wq, wg, wu, we, wo, wd, ck, cv, out, *scratch):
    s = Refs()
    for name, ref in zip(NAMES, scratch):
        setattr(s, name, ref)
    gx = lax.axis_index("gx")
    gy = lax.axis_index("gy")
    yh, core = gx // 2, lax.rem(gx, 2)
    yl, z, x = gy // 16, lax.rem(gy // 4, 4), lax.rem(gy, 4)

    loads = []
    for part in range(2):
        for b in range(4):
            for k, (src, dst) in enumerate(
                ((wq, (s.wq0, s.wq1)), (wg, (s.wg0, s.wg1)), (wu, (s.wu0, s.wu1)))
            ):
                if part == 0:
                    view = src.at[:, b, :, pl.ds(0, PA), :]
                else:
                    view = src.at[:, :, b, pl.ds(PA, PB), :]
                loads.append(pltpu.make_async_copy(view, dst[part].at[b], s.lw.at[part, b, k]))
    rest = [
        pltpu.make_async_copy(a, b, s.lx.at[k])
        for k, (a, b) in enumerate(
            ((we, s.wev), (ck, s.keys), (cv, s.vals), (wd, s.wdv), (wo, s.wov))
        )
    ]
    rest[0].start()
    for cp in loads:
        cp.start()
    for cp in rest[1:]:
        cp.start()

    barrier = pltpu.get_barrier_semaphore()

    def greet(d, carry):
        pl.semaphore_signal(
            barrier,
            inc=1,
            device_id={"gx": gx, "gy": lax.rem(gy + d, 32)},
            device_id_type=pl.DeviceIdType.MESH,
        )
        return carry

    for d in range(1, 4):
        pl.semaphore_signal(
            barrier,
            inc=1,
            device_id={"gx": lax.rem(gx + d, 4), "gy": gy},
            device_id_type=pl.DeviceIdType.MESH,
        )
    lax.fori_loop(1, 32, greet, 0)

    s.pad[...] = jnp.zeros((ROWS, ROWS), F32)
    s.pad[:, 0:COLS] = tok[...].astype(F32)
    turned = s.pad[...].T
    s.pad[...] = turned
    own0 = s.xt0.at[z, yl, x]
    own1 = s.xt1.at[x, yl, z]
    own0[...] = turned[0:PA].astype(BF)
    own1[...] = turned[PA:COLS].astype(BF)
    total = jnp.sum(turned, axis=0, keepdims=True)
    squares = jnp.sum(turned * turned, axis=0, keepdims=True)
    s.st[...] = jnp.zeros((8, 128), F32)
    s.st[0:1, :] = total[:, 0:128]
    s.st[1:2, :] = total[:, 128:256]
    s.st[2:3, :] = squares[:, 0:128]
    s.st[3:4, :] = squares[:, 128:256]

    pl.semaphore_wait(barrier, 34)

    stat_copies = [
        remote(s.st, s.str_.at[d - 1], s.stg.at[0, d - 1], s.stg.at[1, d - 1], lax.rem(gx + d, 4), gy)
        for d in range(1, 4)
    ]
    for cp in stat_copies:
        cp.start()
    first0, first1 = [], []
    for k in range(1, 8):
        dy, dr = k // 4, k % 4
        y2 = lax.rem(yl + dy, 2)
        first0.append(
            remote(own0, own0, s.a0.at[0, k], s.a0.at[1, k], gx, place(y2, z, lax.rem(x + dr, 4)))
        )
        first1.append(
            remote(own1, own1, s.a1.at[0, k], s.a1.at[1, k], gx, place(y2, lax.rem(z + dr, 4), x))
        )
    for p, q in zip(first0, first1):
        p.start()
        q.start()

    s.gpad[...] = jnp.zeros((128, 128), F32)
    s.gpad[0:36, :] = gain[...]
    gain_turned = s.gpad[...].T
    for c in range(36):
        s.gcol[128 * c : 128 * c + 128, :] = jnp.broadcast_to(gain_turned[:, c : c + 1], (128, 128))

    for cp in stat_copies:
        cp.wait_recv()
    s.st2[...] = s.st[...] + s.str_[0] + s.str_[1] + s.str_[2]

    def spread_stats(d, carry):
        p = lax.rem(gy + d, 32)
        remote(s.st2, s.st2r.at[gy], s.sts.at[0], s.sts.at[1], gx, p).start()
        return carry

    lax.fori_loop(1, 32, spread_stats, 0)
    s.st2r[gy] = s.st2[...]

    def fill_length(r, carry):
        s.lenb[pl.ds(r, 1), :] = jnp.full((1, QC), lens[gx * 64 + r].astype(F32), F32)
        return carry

    lax.fori_loop(0, 64, fill_length, 0)
    cosine, sine = rope_tables(s.lenb[...], gy * QC, (64, QC))
    s.cosq[...] = cosine
    s.sinq[...] = sine
    s.pq[...] = jnp.zeros((ROWS, QC), F32)
    s.pg[...] = jnp.zeros((ROWS, FC), F32)
    s.pu[...] = jnp.zeros((ROWS, FC), F32)

    for cp in first0:
        cp.wait_recv()
    second0, second1 = [], []
    for j in range(1, 4):
        second0.append(
            remote(
                s.xt0.at[z], s.xt0.at[z], s.b0.at[0, j], s.b0.at[1, j], gx, place(yl, lax.rem(z + j, 4), x)
            )
        )
        second1.append(
            remote(
                s.xt1.at[x], s.xt1.at[x], s.b1.at[0, j], s.b1.at[1, j], gx, place(yl, z, lax.rem(x + j, 4))
            )
        )
    for cp in second0:
        cp.start()
    for cp in first1:
        cp.wait_recv()
    for cp in second1:
        cp.start()

    many = s.st2r.at[pl.ds(0, 31)]
    pltpu.make_async_copy(many, many, s.sts.at[1]).wait()
    sums = jnp.sum(s.st2r[...], axis=0) * (1.0 / D)
    average = jnp.concatenate([sums[0:1], sums[1:2]], axis=1)
    meansq = jnp.concatenate([sums[2:3], sums[3:4]], axis=1)
    s.stat[0:1, :] = average
    s.stat[1:2, :] = lax.rsqrt(meansq - average * average + EPS)

    def normalize(block, start, rows):
        g = s.gcol[pl.ds(pl.multiple_of(start, 16), rows), :]
        g = jnp.concatenate([g, g], axis=1)
        return ((block.astype(F32) - s.stat[0:1, :]) * s.stat[1:2, :] * g).astype(BF)

    local = normalize(s.pad[0:COLS, :], gy * COLS, COLS)
    rest[0].wait()
    s.pe[...] = dot(local.T, s.wev[...])

    def project(nrm, rows, b, xt, weights, part, shard_of):
        for k in range(3):
            pltpu.make_async_copy(weights[k].at[b], weights[k].at[b], s.lw.at[part, b, k]).wait()

        def one(i, carry):
            a, r = i // 4, lax.rem(i, 4)
            start = shard_of(a, r) * COLS + (0 if part == 0 else PA)
            nrm[pl.ds(pl.multiple_of(i * rows, 16), rows), :] = normalize(xt[b, a, r], start, rows)
            return carry

        lax.fori_loop(0, 8, one, 0)
        lhs = nrm[...].T
        for w, acc in zip(weights, (s.pq, s.pg, s.pu)):
            acc[...] += dot(lhs, w[b].reshape(8 * rows, w.shape[-1]))

    def chunk(j, carry):
        bz = lax.rem(z + 4 - j, 4)
        bx = lax.rem(x + 4 - j, 4)

        @pl.when(j > 0)
        def _():
            pltpu.make_async_copy(s.xt0.at[bz], s.xt0.at[bz], s.b0.at[1, j]).wait()

        project(
            s.nrm0, PA, bz, s.xt0, (s.wq0, s.wg0, s.wu0), 0, lambda a, r: place(a, bz, r)
        )

        @pl.when(j > 0)
        def _():
            pltpu.make_async_copy(s.xt1.at[bx], s.xt1.at[bx], s.b1.at[1, j]).wait()

        project(
            s.nrm1, PB, bx, s.xt1, (s.wq1, s.wg1, s.wu1), 1, lambda a, r: place(a, r, bx)
        )
        return carry

    lax.fori_loop(0, 4, chunk, 0)

    def rows_of(t, c):
        return pl.ds(pl.multiple_of((2 * t + c) * 64, 64), 64)

    for t in range(2):
        give = rows_of(t, 1 - core)
        s.sq1[t, :, 0:QC] = s.pq[give, :].astype(BF)
        s.sq1[t, :, QC:] = s.pe[give, :].astype(BF)
    other_core = yh * 2 + 1 - core
    other_chip = (1 - yh) * 2 + core
    cq1 = remote(s.sq1, s.rq1, s.cq.at[0, 0], s.cq.at[1, 0], other_core, gy)
    cq1.start()
    for t in range(2):
        give = rows_of(t, 1 - core)
        s.sg1[t, 0] = s.pg[give, :].astype(BF)
        s.sg1[t, 1] = s.pu[give, :].astype(BF)
    cg1 = remote(s.sg1, s.rg1, s.cg.at[0, 0], s.cg.at[1, 0], other_core, gy)
    cg1.start()
    cq1.wait_recv()

    def both_cores(t, acc, got):
        return acc[rows_of(t, core), :] + got.astype(F32)

    s.sq2[:, 0:QC] = both_cores(1 - yh, s.pq, s.rq1[1 - yh, :, 0:QC]).astype(BF)
    s.sq2[:, QC:] = both_cores(1 - yh, s.pe, s.rq1[1 - yh, :, QC:]).astype(BF)
    cq2 = remote(s.sq2, s.rq2, s.cq.at[0, 1], s.cq.at[1, 1], other_chip, gy)
    cq2.start()
    cg1.wait_recv()
    s.sg2[0] = both_cores(1 - yh, s.pg, s.rg1[1 - yh, 0]).astype(BF)
    s.sg2[1] = both_cores(1 - yh, s.pu, s.rg1[1 - yh, 1]).astype(BF)
    cg2 = remote(s.sg2, s.rg2, s.cg.at[0, 1], s.cg.at[1, 1], other_chip, gy)
    cg2.start()
    cq2.wait_recv()
    query = both_cores(yh, s.pq, s.rq1[yh, :, 0:QC]) + s.rq2[:, 0:QC].astype(F32)
    query = query * s.cosq[...] + swap_pairs(query) * s.sinq[...]
    entries = both_cores(yh, s.pe, s.rq1[yh, :, QC:]) + s.rq2[:, QC:].astype(F32)
    for k in range(3):
        s.qf[k] = query[:, 128 * k : 128 * k + 128]
    for k in range(4):
        s.ef[k] = entries[:, 128 * k : 128 * k + 128]

    s.msg[...] = jnp.zeros((512, 128), F32)
    for i in range(2):
        for k in range(3):
            s.msg[pl.ds(3 * i + k, 32, stride=16), :] = s.qf[k, pl.ds(i, 32, stride=2), :]
        for k in range(4):
            s.msg[pl.ds(6 + 4 * i + k, 32, stride=16), :] = s.ef[k, pl.ds(i, 32, stride=2), :]
    s.mq[...] = s.msg[...].astype(BF).reshape(32, 16, 128)

    def spread_query(d, carry):
        p = lax.rem(gy + d, 32)
        remote(s.mq.at[p], s.mr.at[gy], s.mqs.at[0], s.mqs.at[1], gx, p).start()
        return carry

    lax.fori_loop(1, 32, spread_query, 0)
    s.mr[gy] = s.mq[gy]

    cg2.wait_recv()
    gate = both_cores(yh, s.pg, s.rg1[yh, 0]) + s.rg2[0].astype(F32)
    up = both_cores(yh, s.pu, s.rg1[yh, 1]) + s.rg2[1].astype(F32)
    s.hidall[gx] = (gate / (1.0 + jnp.exp(-gate)) * up).astype(BF)
    gather_hidden = [
        remote(
            s.hidall.at[gx], s.hidall.at[gx], s.gh.at[0, d - 1], s.gh.at[1, d - 1], lax.rem(gx + d, 4), gy
        )
        for d in range(1, 4)
    ]
    for cp in gather_hidden:
        cp.start()

    many_q = s.mr.at[pl.ds(0, 31)]
    pltpu.make_async_copy(many_q, many_q, s.mqs.at[1]).wait()
    rest[1].wait()
    rest[2].wait()
    s.msg[...] = s.mr[...].reshape(512, 128).astype(F32)
    scale = 1.0 / math.sqrt(DH)
    first_row = (gx * 32 + gy) * 2
    s.aback[...] = jnp.zeros((32, 8, 128), F32)
    replies = []
    for i in range(2):
        for k in range(3):
            s.pieces[pl.ds(k, 32, stride=3), :] = s.msg[pl.ds(3 * i + k, 32, stride=16), :]
        q = jnp.concatenate(
            [s.pieces[pl.ds(0, 48, stride=2), :], s.pieces[pl.ds(1, 48, stride=2), :]], axis=1
        )
        entry = [
            jnp.sum(s.msg[pl.ds(6 + 4 * i + k, 32, stride=16), :], axis=0, keepdims=True)
            for k in range(4)
        ]
        length = lens[first_row + i]
        key = jnp.broadcast_to(jnp.concatenate(entry[0:2], axis=1), (8, DH))
        value = jnp.concatenate(entry[2:4], axis=1).astype(BF).astype(F32)
        key_cos, key_sin = rope_tables(jnp.full((8, DH), length.astype(F32), F32), 0, (8, DH))
        key = (key * key_cos + swap_pairs(key) * key_sin)[0:1].astype(BF).astype(F32)
        qb = q.astype(BF)
        scores = (
            lax.dot_general(qb, s.keys[i], (((1,), (1,)), ((), ())), preferred_element_type=F32) * scale
        )
        position = lax.broadcasted_iota(jnp.int32, (H, CTX), 1)
        scores = jnp.where(position < length, scores, -1e30)
        own = jnp.sum(q * key, axis=1, keepdims=True) * scale
        peak = jnp.maximum(jnp.max(scores, axis=1, keepdims=True), own)
        expd = jnp.exp(scores - peak)
        own_exp = jnp.exp(own - peak)
        denom = jnp.sum(expd, axis=1, keepdims=True) + own_exp
        weights = (expd / denom).astype(BF)
        own_weight = (own_exp / denom).astype(BF).astype(F32)
        mixed = dot(weights, s.vals[i]) + own_weight * value
        s.pieces[pl.ds(0, 48, stride=2), :] = mixed[:, 0:128]
        s.pieces[pl.ds(1, 48, stride=2), :] = mixed[:, 128:256]
        for k in range(3):
            replies.append((3 * i + k, s.pieces[pl.ds(k, 32, stride=3), :]))
    for row, piece in replies:
        s.msg[pl.ds(row, 32, stride=8), :] = piece
    s.aback[...] = s.msg[0:256, :].reshape(32, 8, 128)

    def spread_back(d, carry):
        p = lax.rem(gy + d, 32)
        remote(s.aback.at[p], s.abackr.at[gy], s.abs_.at[0], s.abs_.at[1], gx, p).start()
        return carry

    lax.fori_loop(1, 32, spread_back, 0)
    s.abackr[gy] = s.aback[gy]

    for cp in gather_hidden:
        cp.wait_recv()
    rest[3].wait()

    def down(c, carry):
        cols = pl.ds(pl.multiple_of(c * WIDE, 128), WIDE)
        s.outp[:, cols] = dot(s.hidall[...].reshape(ROWS, FC), s.wdv[:, cols])
        return carry

    lax.fori_loop(0, 4, down, 0)

    many_a = s.abackr.at[pl.ds(0, 31)]
    pltpu.make_async_copy(many_a, many_a, s.abs_.at[1]).wait()
    s.msg[0:256, :] = s.abackr[...].reshape(256, 128)
    for i in range(2):
        for k in range(3):
            s.att64[k, pl.ds(i, 32, stride=2), :] = s.msg[pl.ds(3 * i + k, 32, stride=8), :]
    for k in range(3):
        s.attall[gx, :, 128 * k : 128 * k + 128] = s.att64[k].astype(BF)
    gather_att = [
        remote(
            s.attall.at[gx], s.attall.at[gx], s.ga.at[0, d - 1], s.ga.at[1, d - 1], lax.rem(gx + d, 4), gy
        )
        for d in range(1, 4)
    ]
    for cp in gather_att:
        cp.start()
    rest[4].wait()
    for cp in gather_att:
        cp.wait_recv()

    def finish(c, carry):
        cols = pl.ds(pl.multiple_of(c * WIDE, 128), WIDE)
        v = s.outp[:, cols] + dot(s.attall[...].reshape(ROWS, QC), s.wov[:, cols])
        s.eT[c // 2, pl.ds(lax.rem(c, 2) * 2, 2)] = v.T.astype(BF).reshape(2, 4, COLS, ROWS)
        return carry

    lax.fori_loop(0, 4, finish, 0)

    send0, send1 = [], []
    for j in range(1, 4):
        zz, xx = lax.rem(z + j, 4), lax.rem(x + j, 4)
        send0.append(
            remote(
                s.eT.at[:, zz, :, pl.ds(0, PA), :],
                s.r0.at[j - 1],
                s.e0.at[0, j - 1],
                s.e0.at[1, j - 1],
                gx,
                place(yl, zz, x),
            )
        )
        send1.append(
            remote(
                s.eT.at[:, :, xx, pl.ds(PA, PB), :],
                s.r1.at[j - 1],
                s.e1.at[0, j - 1],
                s.e1.at[1, j - 1],
                gx,
                place(yl, z, xx),
            )
        )
    for p, q in zip(send0, send1):
        p.start()
        q.start()

    for cp in send0:
        cp.wait_recv()

    def add0(i, carry):
        a, r = i // 4, lax.rem(i, 4)
        v = s.eT[a, z, r, 0:PA, :].astype(F32)
        for j in range(3):
            v = v + s.r0[j, a, r].astype(F32)
        s.s0[a, r] = v.astype(BF)
        return carry

    lax.fori_loop(0, 8, add0, 0)
    last0, last1 = [], []
    for k in range(1, 8):
        dy, dr = k // 4, k % 4
        y2, x2, z2 = lax.rem(yl + dy, 2), lax.rem(x + dr, 4), lax.rem(z + dr, 4)
        last0.append(
            remote(s.s0.at[y2, x2], s.r0b.at[k], s.f0.at[0, k], s.f0.at[1, k], gx, place(y2, z, x2))
        )
        last1.append(
            remote(s.s1.at[y2, z2], s.r1b.at[k], s.f1.at[0, k], s.f1.at[1, k], gx, place(y2, z2, x))
        )
    for cp in last0:
        cp.start()
    for cp in send1:
        cp.wait_recv()

    def add1(i, carry):
        a, r = i // 4, lax.rem(i, 4)
        v = s.eT[a, r, x, PA:COLS, :].astype(F32)
        for j in range(3):
            v = v + s.r1[j, a, r].astype(F32)
        s.s1[a, r] = v.astype(BF)
        return carry

    lax.fori_loop(0, 8, add1, 0)
    for cp in last1:
        cp.start()

    s.pad[...] = jnp.zeros((ROWS, ROWS), F32)
    for cp in last0:
        cp.wait_recv()
    v = s.s0[yl, x].astype(F32)
    for k in range(1, 8):
        v = v + s.r0b[k].astype(F32)
    s.pad[0:PA, :] = v
    for cp in last1:
        cp.wait_recv()
    v = s.s1[yl, z].astype(F32)
    for k in range(1, 8):
        v = v + s.r1b[k].astype(F32)
    s.pad[PA:COLS, :] = v
    out[...] = tok[...].astype(F32) + s.pad[...].T[:, 0:COLS]

    for group in (
        stat_copies, first0, first1, second0, second1, (cq1, cg1, cq2, cg2),
        gather_hidden, gather_att, send0, send1, last0, last1,
    ):
        for cp in group:
            cp.wait_send()
    pltpu.make_async_copy(many, many, s.sts.at[0]).wait()
    pltpu.make_async_copy(many_q, many_q, s.mqs.at[0]).wait()
    pltpu.make_async_copy(many_a, many_a, s.abs_.at[0]).wait()


def body(
    tokens, ln_gain, w_query, w_entries, w_out, w_gate, w_up, w_down, cache_keys, cache_values, lengths
):
    split = lambda w: w.reshape(2, 4, 4, COLS, w.shape[1])
    vmem = pl.BlockSpec(memory_space=pltpu.VMEM)
    hbm = pl.BlockSpec(memory_space=pl.ANY)
    return pl.pallas_call(
        kernel,
        out_shape=jax.ShapeDtypeStruct((ROWS, COLS), F32),
        in_specs=[vmem, vmem, pl.BlockSpec(memory_space=pltpu.SMEM)] + [hbm] * 8,
        out_specs=vmem,
        scratch_shapes=[pltpu.VMEM(shape, kind) for shape, kind in SCRATCH.values()]
        + [pltpu.SemaphoreType.DMA(shape) for shape in SEMS.values()],
        compiler_params=pltpu.CompilerParams(
            collective_id=0, has_side_effects=True, vmem_limit_bytes=60 << 20
        ),
        name="layer",
    )(
        tokens,
        ln_gain.reshape(36, 128),
        lengths,
        split(w_query),
        split(w_gate),
        split(w_up),
        w_entries,
        w_out,
        w_down,
        cache_keys,
        cache_values,
    )


def solution(mesh):
    return jax.shard_map(
        body,
        mesh=mesh,
        in_specs=(
            P(None, ("gx", "gy")),
            P("gx"),
            P("gx", "gy"),
            P(("gx", "gy"), None),
            P("gy", "gx"),
            P("gx", "gy"),
            P("gx", "gy"),
            P("gy", "gx"),
            P(("gx", "gy"), None, None),
            P(("gx", "gy"), None, None),
            P(None),
        ),
        out_specs=P(None, ("gx", "gy")),
        check_vma=False,
    )
```

```python
import math

import jax
import jax.numpy as jnp
from jax import lax
from jax.experimental import pallas as pl
from jax.experimental.pallas import tpu as pltpu
from jax.sharding import PartitionSpec as P

D = 18432
H = 48
DH = 256
CTX = 1024
EPS = 1e-05
ROWS = 256
COLS = 144
PA, PB = 80, 64
QC = 384
EC = 512
FC = 576
SLAB = 4608
WIDE = 1152
BF = jnp.bfloat16
F32 = jnp.float32
LOG_BASE = -2.0 * math.log(10000.0) / DH


def dot(a, b):
    return jnp.dot(a, b, preferred_element_type=F32)


def remote(src, dst, send, recv, gx, gy):
    return pltpu.make_async_remote_copy(
        src_ref=src,
        dst_ref=dst,
        send_sem=send,
        recv_sem=recv,
        device_id={"gx": gx, "gy": gy},
        device_id_type=pl.DeviceIdType.MESH,
    )


def place(y, z, x):
    return y * 16 + z * 4 + x


def swap_pairs(v):
    width = v.shape[1]
    even = lax.rem(lax.broadcasted_iota(jnp.int32, v.shape, 1), 2) == 0
    return jnp.where(even, pltpu.roll(v, width - 1, 1), pltpu.roll(v, 1, 1))


def rope_tables(positions, offset, shape):
    col = lax.broadcasted_iota(jnp.int32, shape, 1)
    even = lax.rem(col, 2) == 0
    pair = lax.rem(col + offset, DH) // 2
    angle = positions * jnp.exp(pair.astype(F32) * LOG_BASE)
    sine = jnp.sin(angle)
    return jnp.cos(angle), jnp.where(even, -sine, sine)


SCRATCH = dict(
    wqv=((2, 4, 4, COLS, QC), BF),
    wgv=((2, 4, 4, COLS, FC), BF),
    wuv=((2, 4, 4, COLS, FC), BF),
    turn=((8, FC, WIDE), BF),
    wev=((COLS, EC), BF),
    wov=((QC, SLAB), BF),
    wdv=((FC, SLAB), BF),
    keys=((2, CTX, DH), BF),
    vals=((2, CTX, DH), BF),
    gpad=((128, 128), F32),
    gcol=((SLAB, 128), F32),
    xt0=((4, 2, 4, PA, ROWS), BF),
    xt1=((4, 2, 4, PB, ROWS), BF),
    st=((8, 128), F32),
    str_=((3, 8, 128), F32),
    st2=((8, 128), F32),
    st2r=((7, 8, 128), F32),
    st3=((8, 128), F32),
    st3r=((3, 8, 128), F32),
    stat=((8, ROWS), F32),
    nrm0=((8 * PA, ROWS), BF),
    nrm1=((8 * PB, ROWS), BF),
    pq=((ROWS, QC), F32),
    pe=((ROWS, EC), F32),
    pg=((ROWS, FC), F32),
    pu=((ROWS, FC), F32),
    se1=((2, 64, EC), BF),
    re1=((2, 64, EC), BF),
    se2=((64, EC), BF),
    re2=((64, EC), BF),
    sq1=((2, 64, QC), BF),
    rq1=((2, 64, QC), BF),
    sq2=((64, QC), BF),
    rq2=((64, QC), BF),
    sg1=((2, 2, 64, FC), BF),
    rg1=((2, 2, 64, FC), BF),
    sg2=((2, 64, FC), BF),
    rg2=((2, 64, FC), BF),
    lenb=((64, QC), F32),
    cosq=((64, QC), F32),
    sinq=((64, QC), F32),
    qf=((3, 64, 128), F32),
    ef=((4, 64, 128), F32),
    msg=((512, 128), F32),
    mq=((32, 16, 128), BF),
    mr=((32, 16, 128), BF),
    pieces=((96, 128), F32),
    aback=((32, 8, 128), F32),
    abackr=((32, 8, 128), F32),
    att64=((3, 64, 128), F32),
    attall=((4, 64, QC), BF),
    hidall=((4, 64, FC), BF),
    outp=((ROWS, SLAB), F32),
    eT=((2, 4, 4, COLS, ROWS), BF),
    r0=((3, 2, 4, PA, ROWS), BF),
    r1=((3, 2, 4, PB, ROWS), BF),
    s0=((8, PA, ROWS), BF),
    s1=((8, PB, ROWS), BF),
    r0b=((8, PA, ROWS), BF),
    r1b=((8, PB, ROWS), BF),
)
SEMS = dict(
    lw=(9,),
    lx=(5,),
    stg=(2, 3),
    sts=(2, 7),
    stz=(2, 3),
    a0=(2, 8),
    a1=(2, 8),
    b0=(2, 4),
    b1=(2, 4),
    ce=(2, 2),
    cq=(2, 2),
    cg=(2, 2),
    mqs=(2,),
    abs_=(2,),
    ga=(2, 3),
    gh=(2, 3),
    e0=(2, 3),
    e1=(2, 3),
    f0=(2, 8),
    f1=(2, 8),
)
NAMES = list(SCRATCH) + list(SEMS)


class Refs:
    pass


def kernel(tok, gain, lens, wq, wgt, wut, we, wo, wd, ck, cv, out, *scratch):
    s = Refs()
    for name, ref in zip(NAMES, scratch):
        setattr(s, name, ref)
    gx = lax.axis_index("gx")
    gy = lax.axis_index("gy")
    yh, core = gx // 2, lax.rem(gx, 2)
    yl, z, x = gy // 16, lax.rem(gy // 4, 4), lax.rem(gy, 4)

    loads = []
    for c in range(8):
        src = (wgt, wut)[c // 4].at[:, pl.ds(WIDE * (c % 4), WIDE)]
        loads.append(pltpu.make_async_copy(src, s.turn.at[c], s.lw.at[c]))
    loads.append(pltpu.make_async_copy(wq, s.wqv, s.lw.at[8]))
    rest = [
        pltpu.make_async_copy(a, b, s.lx.at[k])
        for k, (a, b) in enumerate(
            ((we, s.wev), (ck, s.keys), (cv, s.vals), (wd, s.wdv), (wo, s.wov))
        )
    ]
    for cp in loads[:4]:
        cp.start()

    barrier = pltpu.get_barrier_semaphore()

    ring = [lambda d: place(yl, z, lax.rem(x + d, 4)), lambda d: place(yl, lax.rem(z + d, 4), x)]
    plane = [
        lambda k: place(lax.rem(yl + k // 4, 2), z, lax.rem(x + k % 4, 4)),
        lambda k: place(lax.rem(yl + k // 4, 2), lax.rem(z + k % 4, 4), x),
    ]
    greeted = [(lax.rem(gx + d, 4), gy) for d in range(1, 4)]
    greeted += [(gx, plane[0](k)) for k in range(1, 8)]
    greeted += [(gx, plane[1](k)) for k in (1, 2, 3, 5, 6, 7)]
    for to_x, to_y in greeted:
        pl.semaphore_signal(
            barrier, inc=1, device_id={"gx": to_x, "gy": to_y}, device_id_type=pl.DeviceIdType.MESH
        )
    for cp in loads[4:] + rest:
        cp.start()

    own0 = s.xt0.at[z, yl, x]
    own1 = s.xt1.at[x, yl, z]
    own0[...] = tok[0:PA, :]
    own1[...] = tok[PA:COLS, :]
    columns = tok[...].astype(F32)
    total = jnp.sum(columns, axis=0, keepdims=True)
    squares = jnp.sum(columns * columns, axis=0, keepdims=True)
    s.st[...] = jnp.zeros((8, 128), F32)
    s.st[0:1, :] = total[:, 0:128]
    s.st[1:2, :] = total[:, 128:256]
    s.st[2:3, :] = squares[:, 0:128]
    s.st[3:4, :] = squares[:, 128:256]

    def turn_weights(m, dst):
        def one(c, carry):
            at = m * 4 + c
            pltpu.make_async_copy(s.turn.at[at], s.turn.at[at], s.lw.at[at]).wait()
            dst[c // 2, pl.ds(lax.rem(c, 2) * 2, 2)] = s.turn[at].T.reshape(2, 4, COLS, FC)
            return carry

        lax.fori_loop(0, 4, one, 0)

    turn_weights(0, s.wgv)
    pl.semaphore_wait(barrier, len(greeted))

    stat_copies = [
        remote(s.st, s.str_.at[d - 1], s.stg.at[0, d - 1], s.stg.at[1, d - 1], lax.rem(gx + d, 4), gy)
        for d in range(1, 4)
    ]
    for cp in stat_copies:
        cp.start()
    order = (1, 3, 4, 2, 5, 7, 6)
    first0 = {
        k: remote(own0, own0, s.a0.at[0, k], s.a0.at[1, k], gx, plane[0](k)) for k in order
    }
    first1 = {
        k: remote(own1, own1, s.a1.at[0, k], s.a1.at[1, k], gx, plane[1](k)) for k in order
    }
    for k in order:
        first0[k].start()
        first1[k].start()

    def forward0(k):
        a, r = lax.rem(yl + k // 4, 2), lax.rem(x + 4 - k % 4, 4)
        piece = s.xt0.at[z, a, r]
        for j in (1, 3, 2):
            remote(piece, piece, s.b0.at[0, j], s.b0.at[1, j], gx, ring[1](j)).start()

    def forward1(k):
        a, r = lax.rem(yl + k // 4, 2), lax.rem(z + 4 - k % 4, 4)
        piece = s.xt1.at[x, a, r]
        for j in (1, 3, 2):
            remote(piece, piece, s.b1.at[0, j], s.b1.at[1, j], gx, ring[0](j)).start()

    forward0(0)
    forward1(0)

    s.gpad[...] = jnp.zeros((128, 128), F32)
    s.gpad[0:36, :] = gain[...]
    gain_turned = s.gpad[...].T
    for c in range(36):
        s.gcol[128 * c : 128 * c + 128, :] = jnp.broadcast_to(gain_turned[:, c : c + 1], (128, 128))

    for cp in stat_copies:
        cp.wait_recv()
    s.st2[...] = s.st[...] + s.str_[0] + s.str_[1] + s.str_[2]

    spread_stats = [
        remote(s.st2, s.st2r.at[k - 1], s.sts.at[0, k - 1], s.sts.at[1, k - 1], gx, plane[0](k))
        for k in range(1, 8)
    ]
    for cp in spread_stats:
        cp.start()
    for k in order[:3]:
        first0[k].wait_recv()
        forward0(k)
        first1[k].wait_recv()
        forward1(k)

    def fill_length(r, carry):
        s.lenb[pl.ds(r, 1), :] = jnp.full((1, QC), lens[gx * 64 + r].astype(F32), F32)
        return carry

    lax.fori_loop(0, 64, fill_length, 0)
    cosine, sine = rope_tables(s.lenb[...], gy * QC, (64, QC))
    s.cosq[...] = cosine
    s.sinq[...] = sine
    s.pq[...] = jnp.zeros((ROWS, QC), F32)
    s.pg[...] = jnp.zeros((ROWS, FC), F32)
    s.pu[...] = jnp.zeros((ROWS, FC), F32)

    for k in order[3:]:
        first0[k].wait_recv()
        forward0(k)
        first1[k].wait_recv()
        forward1(k)

    for cp in spread_stats:
        cp.wait_recv()
    s.st3[...] = s.st2[...] + jnp.sum(s.st2r[...], axis=0)
    last_stats = [
        remote(s.st3, s.st3r.at[j - 1], s.stz.at[0, j - 1], s.stz.at[1, j - 1], gx, ring[1](j))
        for j in range(1, 4)
    ]
    for cp in last_stats:
        cp.start()
    turn_weights(1, s.wuv)
    for cp in last_stats:
        cp.wait_recv()
    sums = (s.st3[...] + jnp.sum(s.st3r[...], axis=0)) * (1.0 / D)
    average = jnp.concatenate([sums[0:1], sums[1:2]], axis=1)
    meansq = jnp.concatenate([sums[2:3], sums[3:4]], axis=1)
    s.stat[0:1, :] = average
    s.stat[1:2, :] = lax.rsqrt(meansq - average * average + EPS)

    def normalize(block, start, rows):
        g = s.gcol[pl.ds(pl.multiple_of(start, 16), rows), :]
        g = jnp.concatenate([g, g], axis=1)
        return ((block.astype(F32) - s.stat[0:1, :]) * s.stat[1:2, :] * g).astype(BF)

    local = normalize(tok[...], gy * COLS, COLS)
    rest[0].wait()
    s.pe[...] = dot(local.T, s.wev[...])

    def rows_of(t, c):
        return pl.ds(pl.multiple_of((2 * t + c) * 64, 64), 64)

    def both_cores(t, acc, got):
        return acc[rows_of(t, core), :] + got.astype(F32)

    other_core = yh * 2 + 1 - core
    other_chip = (1 - yh) * 2 + core
    for t in range(2):
        s.se1[t] = s.pe[rows_of(t, 1 - core), :].astype(BF)
    ce1 = remote(s.se1, s.re1, s.ce.at[0, 0], s.ce.at[1, 0], other_core, gy)
    ce2 = remote(s.se2, s.re2, s.ce.at[0, 1], s.ce.at[1, 1], other_chip, gy)
    ce1.start()

    weights = ((s.wqv, s.pq), (s.wgv, s.pg), (s.wuv, s.pu))
    loads[8].wait()

    def project(nrm, rows, b, xt, part, shard_of):
        def one(i, carry):
            a, r = i // 4, lax.rem(i, 4)
            start = shard_of(a, r) * COLS + (0 if part == 0 else PA)
            nrm[pl.ds(pl.multiple_of(i * rows, 16), rows), :] = normalize(xt[b, a, r], start, rows)
            return carry

        lax.fori_loop(0, 8, one, 0)
        lhs = nrm[...].T
        for w, acc in weights:
            rhs = w[:, b, :, 0:PA, :] if part == 0 else w[:, :, b, PA:COLS, :]
            acc[...] += dot(lhs, rhs.reshape(8 * rows, w.shape[-1]))

    def chunk(j, carry):
        bz = lax.rem(z + 4 - j, 4)
        bx = lax.rem(x + 4 - j, 4)

        @pl.when(j > 0)
        def _():
            pltpu.make_async_copy(s.xt0.at[bz], s.xt0.at[bz], s.b0.at[1, j]).wait()

        project(s.nrm0, PA, bz, s.xt0, 0, lambda a, r: place(a, bz, r))

        @pl.when(j > 0)
        def _():
            pltpu.make_async_copy(s.xt1.at[bx], s.xt1.at[bx], s.b1.at[1, j]).wait()

        project(s.nrm1, PB, bx, s.xt1, 1, lambda a, r: place(a, r, bx))

        @pl.when(j == 0)
        def _():
            ce1.wait_recv()
            s.se2[...] = both_cores(1 - yh, s.pe, s.re1[1 - yh]).astype(BF)
            ce2.start()

        return carry

    lax.fori_loop(0, 4, chunk, 0)

    for t in range(2):
        give = rows_of(t, 1 - core)
        s.sq1[t] = s.pq[give, :].astype(BF)
    cq1 = remote(s.sq1, s.rq1, s.cq.at[0, 0], s.cq.at[1, 0], other_core, gy)
    cq1.start()
    for t in range(2):
        give = rows_of(t, 1 - core)
        s.sg1[t, 0] = s.pg[give, :].astype(BF)
        s.sg1[t, 1] = s.pu[give, :].astype(BF)
    cg1 = remote(s.sg1, s.rg1, s.cg.at[0, 0], s.cg.at[1, 0], other_core, gy)
    cg1.start()
    cq1.wait_recv()

    s.sq2[...] = both_cores(1 - yh, s.pq, s.rq1[1 - yh]).astype(BF)
    cq2 = remote(s.sq2, s.rq2, s.cq.at[0, 1], s.cq.at[1, 1], other_chip, gy)
    cq2.start()
    cg1.wait_recv()
    s.sg2[0] = both_cores(1 - yh, s.pg, s.rg1[1 - yh, 0]).astype(BF)
    s.sg2[1] = both_cores(1 - yh, s.pu, s.rg1[1 - yh, 1]).astype(BF)
    cg2 = remote(s.sg2, s.rg2, s.cg.at[0, 1], s.cg.at[1, 1], other_chip, gy)
    cg2.start()
    ce2.wait_recv()
    entries = both_cores(yh, s.pe, s.re1[yh]) + s.re2[...].astype(F32)
    for k in range(4):
        s.ef[k] = entries[:, 128 * k : 128 * k + 128]
    s.msg[...] = jnp.zeros((512, 128), F32)
    for i in range(2):
        for k in range(4):
            s.msg[pl.ds(6 + 4 * i + k, 32, stride=16), :] = s.ef[k, pl.ds(i, 32, stride=2), :]
    cq2.wait_recv()
    query = both_cores(yh, s.pq, s.rq1[yh]) + s.rq2[...].astype(F32)
    query = query * s.cosq[...] + swap_pairs(query) * s.sinq[...]
    for k in range(3):
        s.qf[k] = query[:, 128 * k : 128 * k + 128]

    for i in range(2):
        for k in range(3):
            s.msg[pl.ds(3 * i + k, 32, stride=16), :] = s.qf[k, pl.ds(i, 32, stride=2), :]
    s.mq[...] = s.msg[...].astype(BF).reshape(32, 16, 128)

    def spread_query(d, carry):
        p = lax.rem(gy + d, 32)
        remote(s.mq.at[p], s.mr.at[gy], s.mqs.at[0], s.mqs.at[1], gx, p).start()
        return carry

    lax.fori_loop(1, 32, spread_query, 0)
    s.mr[gy] = s.mq[gy]

    cg2.wait_recv()
    gate = both_cores(yh, s.pg, s.rg1[yh, 0]) + s.rg2[0].astype(F32)
    up = both_cores(yh, s.pu, s.rg1[yh, 1]) + s.rg2[1].astype(F32)
    s.hidall[gx] = (gate / (1.0 + jnp.exp(-gate)) * up).astype(BF)
    gather_hidden = [
        remote(
            s.hidall.at[gx], s.hidall.at[gx], s.gh.at[0, d - 1], s.gh.at[1, d - 1], lax.rem(gx + d, 4), gy
        )
        for d in range(1, 4)
    ]
    for cp in gather_hidden:
        cp.start()

    many_q = s.mr.at[pl.ds(0, 31)]
    pltpu.make_async_copy(many_q, many_q, s.mqs.at[1]).wait()
    rest[1].wait()
    rest[2].wait()
    s.msg[...] = s.mr[...].reshape(512, 128).astype(F32)
    scale = 1.0 / math.sqrt(DH)
    first_row = (gx * 32 + gy) * 2
    s.aback[...] = jnp.zeros((32, 8, 128), F32)
    replies = []
    for i in range(2):
        for k in range(3):
            s.pieces[pl.ds(k, 32, stride=3), :] = s.msg[pl.ds(3 * i + k, 32, stride=16), :]
        q = jnp.concatenate(
            [s.pieces[pl.ds(0, 48, stride=2), :], s.pieces[pl.ds(1, 48, stride=2), :]], axis=1
        )
        entry = [
            jnp.sum(s.msg[pl.ds(6 + 4 * i + k, 32, stride=16), :], axis=0, keepdims=True)
            for k in range(4)
        ]
        length = lens[first_row + i]
        key = jnp.broadcast_to(jnp.concatenate(entry[0:2], axis=1), (8, DH))
        value = jnp.concatenate(entry[2:4], axis=1).astype(BF).astype(F32)
        key_cos, key_sin = rope_tables(jnp.full((8, DH), length.astype(F32), F32), 0, (8, DH))
        key = (key * key_cos + swap_pairs(key) * key_sin)[0:1].astype(BF).astype(F32)
        qb = q.astype(BF)
        scores = (
            lax.dot_general(qb, s.keys[i], (((1,), (1,)), ((), ())), preferred_element_type=F32) * scale
        )
        position = lax.broadcasted_iota(jnp.int32, (H, CTX), 1)
        scores = jnp.where(position < length, scores, -1e30)
        own = jnp.sum(q * key, axis=1, keepdims=True) * scale
        peak = jnp.maximum(jnp.max(scores, axis=1, keepdims=True), own)
        expd = jnp.exp(scores - peak)
        own_exp = jnp.exp(own - peak)
        denom = jnp.sum(expd, axis=1, keepdims=True) + own_exp
        weights = (expd / denom).astype(BF)
        own_weight = (own_exp / denom).astype(BF).astype(F32)
        mixed = dot(weights, s.vals[i]) + own_weight * value
        s.pieces[pl.ds(0, 48, stride=2), :] = mixed[:, 0:128]
        s.pieces[pl.ds(1, 48, stride=2), :] = mixed[:, 128:256]
        for k in range(3):
            replies.append((3 * i + k, s.pieces[pl.ds(k, 32, stride=3), :]))
    for row, piece in replies:
        s.msg[pl.ds(row, 32, stride=8), :] = piece
    s.aback[...] = s.msg[0:256, :].reshape(32, 8, 128)

    def spread_back(d, carry):
        p = lax.rem(gy + d, 32)
        remote(s.aback.at[p], s.abackr.at[gy], s.abs_.at[0], s.abs_.at[1], gx, p).start()
        return carry

    lax.fori_loop(1, 32, spread_back, 0)
    s.abackr[gy] = s.aback[gy]

    for cp in gather_hidden:
        cp.wait_recv()
    rest[3].wait()

    def down(c, carry):
        cols = pl.ds(pl.multiple_of(c * WIDE, 128), WIDE)
        s.outp[:, cols] = dot(s.hidall[...].reshape(ROWS, FC), s.wdv[:, cols])
        return carry

    lax.fori_loop(0, 4, down, 0)

    many_a = s.abackr.at[pl.ds(0, 31)]
    pltpu.make_async_copy(many_a, many_a, s.abs_.at[1]).wait()
    s.msg[0:256, :] = s.abackr[...].reshape(256, 128)
    for i in range(2):
        for k in range(3):
            s.att64[k, pl.ds(i, 32, stride=2), :] = s.msg[pl.ds(3 * i + k, 32, stride=8), :]
    for k in range(3):
        s.attall[gx, :, 128 * k : 128 * k + 128] = s.att64[k].astype(BF)
    gather_att = [
        remote(
            s.attall.at[gx], s.attall.at[gx], s.ga.at[0, d - 1], s.ga.at[1, d - 1], lax.rem(gx + d, 4), gy
        )
        for d in range(1, 4)
    ]
    for cp in gather_att:
        cp.start()
    rest[4].wait()
    for cp in gather_att:
        cp.wait_recv()

    def send0(zz):
        j = lax.rem(zz - z + 4, 4)
        return remote(
            s.eT.at[:, zz, :, pl.ds(0, PA), :],
            s.r0.at[j - 1],
            s.e0.at[0, j - 1],
            s.e0.at[1, j - 1],
            gx,
            place(yl, zz, x),
        )

    def send1(j, pair):
        return remote(
            s.eT.at[:, pl.ds(2 * pair, 2), lax.rem(x + j, 4), pl.ds(PA, PB), :],
            s.r1.at[j - 1, :, pl.ds(2 * pair, 2)],
            s.e1.at[0, j - 1],
            s.e1.at[1, j - 1],
            gx,
            ring[0](j),
        )

    for half in range(2):
        pair = lax.rem(z // 2 + 1 + half, 2)

        def finish(a, carry):
            cols = pl.ds(pl.multiple_of((2 * a + pair) * WIDE, 128), WIDE)
            v = s.outp[:, cols] + dot(s.attall[...].reshape(ROWS, QC), s.wov[:, cols])
            s.eT[a, pl.ds(pair * 2, 2)] = v.T.astype(BF).reshape(2, 4, COLS, ROWS)
            return carry

        lax.fori_loop(0, 2, finish, 0)
        if half == 0:
            send0(2 * pair).start()
            send0(2 * pair + 1).start()
        else:
            send0(2 * pair + 1 - lax.rem(z, 2)).start()
        for j in (1, 3, 2):
            send1(j, pair).start()

    for j in range(3):
        pltpu.make_async_copy(s.r0.at[j], s.r0.at[j], s.e0.at[1, j]).wait()
    last0 = {
        k: remote(
            s.s0.at[k], s.r0b.at[k], s.f0.at[0, k], s.f0.at[1, k], gx, plane[0](k)
        )
        for k in order
    }
    last1 = {
        k: remote(
            s.s1.at[k], s.r1b.at[k], s.f1.at[0, k], s.f1.at[1, k], gx, plane[1](k)
        )
        for k in order
    }

    def add0(k):
        a, r = lax.rem(yl + k // 4, 2), lax.rem(x + k % 4, 4)
        v = s.eT[a, z, r, 0:PA, :].astype(F32)
        for j in range(3):
            v = v + s.r0[j, a, r].astype(F32)
        return v

    def add1(k):
        a, r = lax.rem(yl + k // 4, 2), lax.rem(z + k % 4, 4)
        v = s.eT[a, r, x, PA:COLS, :].astype(F32)
        for j in range(3):
            v = v + s.r1[j, a, r].astype(F32)
        return v

    for k in order:
        s.s0[k] = add0(k).astype(BF)
        last0[k].start()
    for j in range(3):
        pltpu.make_async_copy(s.r1.at[j], s.r1.at[j], s.e1.at[1, j]).wait()
    for k in order:
        s.s1[k] = add1(k).astype(BF)
        last1[k].start()
    v0 = tok[0:PA, :].astype(F32) + add0(0)
    v1 = tok[PA:COLS, :].astype(F32) + add1(0)
    for k in order:
        last0[k].wait_recv()
        v0 = v0 + s.r0b[k].astype(F32)
    out[0:PA, :] = v0
    for k in order:
        last1[k].wait_recv()
        v1 = v1 + s.r1b[k].astype(F32)
    out[PA:COLS, :] = v1

    for group in (
        stat_copies, spread_stats, last_stats, (ce1, ce2, cq1, cg1, cq2, cg2),
        gather_hidden, gather_att, first0.values(), first1.values(), last0.values(), last1.values(),
    ):
        for cp in group:
            cp.wait_send()
    for j in range(1, 4):
        pltpu.make_async_copy(s.xt0.at[z], s.xt0.at[z], s.b0.at[0, j]).wait()
        pltpu.make_async_copy(s.xt1.at[x], s.xt1.at[x], s.b1.at[0, j]).wait()
    for j in range(3):
        pltpu.make_async_copy(s.r0.at[j], s.r0.at[j], s.e0.at[0, j]).wait()
        pltpu.make_async_copy(s.r1.at[j], s.r1.at[j], s.e1.at[0, j]).wait()
    pltpu.make_async_copy(many_q, many_q, s.mqs.at[0]).wait()
    pltpu.make_async_copy(many_a, many_a, s.abs_.at[0]).wait()


def body(
    tokens, ln_gain, w_query, w_entries, w_out, w_gate, w_up, w_down, cache_keys, cache_values, lengths
):
    vmem = pl.BlockSpec(memory_space=pltpu.VMEM)
    hbm = pl.BlockSpec(memory_space=pl.ANY)
    return pl.pallas_call(
        kernel,
        out_shape=jax.ShapeDtypeStruct((COLS, ROWS), F32),
        in_specs=[vmem, vmem, pl.BlockSpec(memory_space=pltpu.SMEM)] + [hbm] * 8,
        out_specs=vmem,
        scratch_shapes=[pltpu.VMEM(shape, kind) for shape, kind in SCRATCH.values()]
        + [pltpu.SemaphoreType.DMA(shape) for shape in SEMS.values()],
        compiler_params=pltpu.CompilerParams(
            collective_id=0, has_side_effects=True, vmem_limit_bytes=60 << 20
        ),
        name="layer",
    )(
        tokens.T,
        ln_gain.reshape(36, 128),
        lengths,
        w_query.reshape(2, 4, 4, COLS, QC),
        w_gate.T,
        w_up.T,
        w_entries,
        w_out,
        w_down,
        cache_keys,
        cache_values,
    ).T


def solution(mesh):
    return jax.shard_map(
        body,
        mesh=mesh,
        in_specs=(
            P(None, ("gx", "gy")),
            P("gx"),
            P("gx", "gy"),
            P(("gx", "gy"), None),
            P("gy", "gx"),
            P("gx", "gy"),
            P("gx", "gy"),
            P("gy", "gx"),
            P(("gx", "gy"), None, None),
            P(("gx", "gy"), None, None),
            P(None),
        ),
        out_specs=P(None, ("gx", "gy")),
        check_vma=False,
    )
```

```python
import math

import jax
import jax.numpy as jnp
from jax import lax
from jax.experimental import pallas as pl
from jax.experimental.pallas import tpu as pltpu
from jax.sharding import PartitionSpec as P

D = 18432
H = 48
DH = 256
CTX = 1024
EPS = 1e-05
ROWS = 256
COLS = 144
PA, PB = 80, 64
QC = 384
EC = 512
FC = 576
SLAB = 4608
WIDE = 1152
BF = jnp.bfloat16
F32 = jnp.float32
LOG_BASE = -2.0 * math.log(10000.0) / DH


def dot(a, b):
    return jnp.dot(a, b, preferred_element_type=F32)


def remote(src, dst, send, recv, gx, gy):
    return pltpu.make_async_remote_copy(
        src_ref=src,
        dst_ref=dst,
        send_sem=send,
        recv_sem=recv,
        device_id={"gx": gx, "gy": gy},
        device_id_type=pl.DeviceIdType.MESH,
    )


def place(y, z, x):
    return y * 16 + z * 4 + x


def swap_pairs(v):
    width = v.shape[1]
    even = lax.rem(lax.broadcasted_iota(jnp.int32, v.shape, 1), 2) == 0
    return jnp.where(even, pltpu.roll(v, width - 1, 1), pltpu.roll(v, 1, 1))


def rope_tables(positions, offset, shape):
    col = lax.broadcasted_iota(jnp.int32, shape, 1)
    even = lax.rem(col, 2) == 0
    pair = lax.rem(col + offset, DH) // 2
    angle = positions * jnp.exp(pair.astype(F32) * LOG_BASE)
    sine = jnp.sin(angle)
    return jnp.cos(angle), jnp.where(even, -sine, sine)


SCRATCH = dict(
    wqv=((2, 4, 4, COLS, QC), BF),
    wgv=((2, 4, 4, COLS, FC), BF),
    wuv=((2, 4, 4, COLS, FC), BF),
    turn=((8, FC, WIDE), BF),
    wev=((COLS, EC), BF),
    wov=((QC, SLAB), BF),
    wdv=((FC, SLAB), BF),
    keys=((2, CTX, DH), BF),
    vals=((2, CTX, DH), BF),
    gpad=((128, 128), F32),
    gcol=((SLAB, 128), F32),
    xt0=((4, 2, 4, PA, ROWS), BF),
    xt1=((4, 2, 4, PB, ROWS), BF),
    st=((8, 128), F32),
    str_=((3, 8, 128), F32),
    st2=((8, 128), F32),
    st2r=((7, 8, 128), F32),
    st3=((8, 128), F32),
    st3r=((3, 8, 128), F32),
    stat=((8, ROWS), F32),
    nrm0=((8 * PA, ROWS), BF),
    nrm1=((8 * PB, ROWS), BF),
    pq=((ROWS, QC), F32),
    pe=((ROWS, EC), F32),
    pg=((ROWS, FC), F32),
    pu=((ROWS, FC), F32),
    se1=((2, 64, EC), BF),
    re1=((2, 64, EC), BF),
    se2=((64, EC), BF),
    re2=((64, EC), BF),
    sq1=((2, 64, QC), BF),
    rq1=((2, 64, QC), BF),
    sq2=((64, QC), BF),
    rq2=((64, QC), BF),
    sg1=((2, 2, 64, FC), BF),
    rg1=((2, 2, 64, FC), BF),
    sg2=((2, 64, FC), BF),
    rg2=((2, 64, FC), BF),
    lenb=((64, QC), F32),
    cosq=((64, QC), F32),
    sinq=((64, QC), F32),
    qf=((3, 64, 128), F32),
    ef=((4, 64, 128), F32),
    msg=((512, 128), F32),
    mq=((32, 16, 128), BF),
    mr=((32, 16, 128), BF),
    pieces=((96, 128), F32),
    aback=((32, 8, 128), F32),
    abackr=((32, 8, 128), F32),
    att64=((3, 64, 128), F32),
    attall=((4, 64, QC), BF),
    hidall=((4, 64, FC), BF),
    outp=((ROWS, SLAB), F32),
    eT=((2, 4, 4, COLS, ROWS), BF),
    r0=((2, 2, 4, PA, ROWS), BF),
    r1=((2, 2, 4, PB, ROWS), BF),
    y0=((2, 4, PA, ROWS), BF),
    y1=((2, 4, PB, ROWS), BF),
    c0=((2, 4, PA, ROWS), BF),
    c1=((2, 4, PB, ROWS), BF),
    s0=((8, PA, ROWS), BF),
    s1=((8, PB, ROWS), BF),
    r0b=((8, PA, ROWS), BF),
    r1b=((8, PB, ROWS), BF),
)
SEMS = dict(
    lw=(9,),
    lx=(5,),
    stg=(2, 3),
    sts=(2, 7),
    stz=(2, 3),
    a0=(2, 8),
    a1=(2, 8),
    b0=(2, 4, 4),
    b1=(2, 4, 4),
    ce=(2, 2),
    cq=(2, 2),
    cg=(2, 2),
    mqs=(2,),
    abs_=(2,),
    ga=(2, 3),
    gh=(2, 3),
    e0=(2, 3, 2, 4),
    e1=(2, 3, 2, 4),
    f0=(2, 8),
    f1=(2, 8),
)
NAMES = list(SCRATCH) + list(SEMS)


class Refs:
    pass


def kernel(tok, gain, lens, wq, wgt, wut, we, wo, wd, ck, cv, out, *scratch):
    s = Refs()
    for name, ref in zip(NAMES, scratch):
        setattr(s, name, ref)
    gx = lax.axis_index("gx")
    gy = lax.axis_index("gy")
    yh, core = gx // 2, lax.rem(gx, 2)
    yl, z, x = gy // 16, lax.rem(gy // 4, 4), lax.rem(gy, 4)

    barrier = pltpu.get_barrier_semaphore()

    ring = [lambda d: place(yl, z, lax.rem(x + d, 4)), lambda d: place(yl, lax.rem(z + d, 4), x)]
    plane = [
        lambda k: place(lax.rem(yl + k // 4, 2), z, lax.rem(x + k % 4, 4)),
        lambda k: place(lax.rem(yl + k // 4, 2), lax.rem(z + k % 4, 4), x),
    ]
    far = (2, 1, 3, 0)
    others = [
        place(lax.rem(yl + dy, 2), lax.rem(z + dz, 4), lax.rem(x + dx, 4))
        for dy in (1, 0)
        for dz in far
        for dx in far
    ][:-1]
    greeted = [(lax.rem(gx + d, 4), gy) for d in range(1, 4)]
    greeted += [(gx, plane[0](k)) for k in range(1, 8)]
    greeted += [(gx, plane[1](k)) for k in (1, 2, 3, 5, 6, 7)]
    for to_x, to_y in greeted:
        pl.semaphore_signal(
            barrier, inc=1, device_id={"gx": to_x, "gy": to_y}, device_id_type=pl.DeviceIdType.MESH
        )
    loads = []
    for c in range(8):
        src = (wgt, wut)[c // 4].at[:, pl.ds(WIDE * (c % 4), WIDE)]
        loads.append(pltpu.make_async_copy(src, s.turn.at[c], s.lw.at[c]))
    loads.append(pltpu.make_async_copy(wq, s.wqv, s.lw.at[8]))
    rest = [
        pltpu.make_async_copy(a, b, s.lx.at[k])
        for k, (a, b) in enumerate(
            ((we, s.wev), (ck, s.keys), (cv, s.vals), (wd, s.wdv), (wo, s.wov))
        )
    ]
    for cp in loads + rest:
        cp.start()

    own0 = s.xt0.at[z, yl, x]
    own1 = s.xt1.at[x, yl, z]
    own0[...] = tok[0:PA, :]
    own1[...] = tok[PA:COLS, :]
    columns = tok[...].astype(F32)
    total = jnp.sum(columns, axis=0, keepdims=True)
    squares = jnp.sum(columns * columns, axis=0, keepdims=True)
    s.st[...] = jnp.zeros((8, 128), F32)
    s.st[0:1, :] = total[:, 0:128]
    s.st[1:2, :] = total[:, 128:256]
    s.st[2:3, :] = squares[:, 0:128]
    s.st[3:4, :] = squares[:, 128:256]

    def turn_weights(m, dst):
        def one(c, carry):
            at = m * 4 + c
            pltpu.make_async_copy(s.turn.at[at], s.turn.at[at], s.lw.at[at]).wait()
            dst[c // 2, pl.ds(lax.rem(c, 2) * 2, 2)] = s.turn[at].T.reshape(2, 4, COLS, FC)
            return carry

        lax.fori_loop(0, 4, one, 0)

    turn_weights(0, s.wgv)
    pl.semaphore_wait(barrier, len(greeted))

    stat_z = [
        remote(s.st, s.str_.at[j - 1], s.stg.at[0, j - 1], s.stg.at[1, j - 1], gx, ring[1](j))
        for j in range(1, 4)
    ]
    for cp in stat_z:
        cp.start()
    order = (4, 1, 5, 3, 7, 2, 6)
    first0 = {
        k: remote(own0, own0, s.a0.at[0, k], s.a0.at[1, k], gx, plane[0](k)) for k in order
    }
    first1 = {
        k: remote(own1, own1, s.a1.at[0, k], s.a1.at[1, k], gx, plane[1](k)) for k in order
    }
    for k in order:
        first0[k].start()
        first1[k].start()

    xts, bs, parts = (s.xt0, s.xt1), (s.b0, s.b1), ((0, PA), (PA, PB))

    def shard(part, ring_at, dy, dr):
        a = lax.rem(yl + dy, 2)
        return xts[part].at[ring_at, a, lax.rem((x, z)[part] + 4 - dr, 4)]

    def along(part, d):
        return lax.rem((z, x)[part] + d, 4)

    def forward(k):
        group = (0, 1, 3, 2)[k % 4]
        for part in range(2):
            if k > 0:
                (first0, first1)[part][k].wait_recv()
            piece = shard(part, along(part, 0), k // 4, k % 4)
            for j in (1, 3):
                remote(
                    piece, piece, bs[part].at[0, j, group], bs[part].at[1, j, group], gx, ring[1 - part](j)
                ).start()

    def arrived(part, j, group):
        two = xts[part].at[0, 0, pl.ds(0, 2)]
        pltpu.make_async_copy(two, two, bs[part].at[1, j, group]).wait()

    def hand_on(group):
        dr = group + group // 2 - 2 * (group // 3)
        for part in range(2):
            for j, back, dy in ((1, 3, 0), (3, 1, 1)):
                arrived(part, j, group)
                piece = shard(part, along(part, back), dy, dr)
                remote(
                    piece, piece, bs[part].at[0, 2, group], bs[part].at[1, 2, group], gx, ring[1 - part](j)
                ).start()

    for cp in stat_z:
        cp.wait_recv()
    s.st2[...] = s.st[...] + s.str_[0] + s.str_[1] + s.str_[2]
    stat_plane = [
        remote(s.st2, s.st2r.at[k - 1], s.sts.at[0, k - 1], s.sts.at[1, k - 1], gx, plane[0](k))
        for k in range(1, 8)
    ]
    for cp in stat_plane:
        cp.start()
    forward(0)

    s.gpad[...] = jnp.zeros((128, 128), F32)
    s.gpad[0:36, :] = gain[...]
    gain_turned = s.gpad[...].T
    for c in range(36):
        s.gcol[128 * c : 128 * c + 128, :] = jnp.broadcast_to(gain_turned[:, c : c + 1], (128, 128))

    for k in order[:3]:
        forward(k)

    def fill_length(r, carry):
        s.lenb[pl.ds(r, 1), :] = jnp.full((1, QC), lens[gx * 64 + r].astype(F32), F32)
        return carry

    lax.fori_loop(0, 64, fill_length, 0)
    cosine, sine = rope_tables(s.lenb[...], gy * QC, (64, QC))
    s.cosq[...] = cosine
    s.sinq[...] = sine
    s.pq[...] = jnp.zeros((ROWS, QC), F32)
    s.pg[...] = jnp.zeros((ROWS, FC), F32)
    s.pu[...] = jnp.zeros((ROWS, FC), F32)

    for cp in stat_plane:
        cp.wait_recv()
    s.st3[...] = s.st2[...] + jnp.sum(s.st2r[...], axis=0)
    stat_gx = [
        remote(s.st3, s.st3r.at[d - 1], s.stz.at[0, d - 1], s.stz.at[1, d - 1], lax.rem(gx + d, 4), gy)
        for d in range(1, 4)
    ]
    for cp in stat_gx:
        cp.start()
    for k in order[3:]:
        forward(k)
    turn_weights(1, s.wuv)
    for cp in stat_gx:
        cp.wait_recv()
    sums = (s.st3[...] + jnp.sum(s.st3r[...], axis=0)) * (1.0 / D)
    average = jnp.concatenate([sums[0:1], sums[1:2]], axis=1)
    meansq = jnp.concatenate([sums[2:3], sums[3:4]], axis=1)
    s.stat[0:1, :] = average
    s.stat[1:2, :] = lax.rsqrt(meansq - average * average + EPS)

    def normalize(block, start, rows):
        g = s.gcol[pl.ds(pl.multiple_of(start, 16), rows), :]
        g = jnp.concatenate([g, g], axis=1)
        return ((block.astype(F32) - s.stat[0:1, :]) * s.stat[1:2, :] * g).astype(BF)

    local = normalize(tok[...], gy * COLS, COLS)
    rest[0].wait()
    s.pe[...] = dot(local.T, s.wev[...])

    def rows_of(t, c):
        return pl.ds(pl.multiple_of((2 * t + c) * 64, 64), 64)

    def both_cores(t, acc, got):
        return acc[rows_of(t, core), :] + got.astype(F32)

    other_core = yh * 2 + 1 - core
    other_chip = (1 - yh) * 2 + core
    for t in range(2):
        s.se1[t] = s.pe[rows_of(t, 1 - core), :].astype(BF)
    ce1 = remote(s.se1, s.re1, s.ce.at[0, 0], s.ce.at[1, 0], other_core, gy)
    ce2 = remote(s.se2, s.re2, s.ce.at[0, 1], s.ce.at[1, 1], other_chip, gy)
    ce1.start()

    weights = ((s.wqv, s.pq), (s.wgv, s.pg), (s.wuv, s.pu))
    loads[8].wait()

    def project(nrm, part, group):
        start, rows = parts[part]
        dr = group + group // 2 - 2 * (group // 3)
        spots = []
        for i in range(8):
            a = lax.rem(yl + i % 2, 2)
            r = lax.rem((x, z)[part] + 4 - dr, 4)
            spots.append((a, i // 2, r) if part == 0 else (a, r, i // 2))
        for i, (a, zz, xx) in enumerate(spots):
            block = s.xt0[zz, a, xx] if part == 0 else s.xt1[xx, a, zz]
            nrm[i * rows : (i + 1) * rows, :] = normalize(block, place(a, zz, xx) * COLS + start, rows)
        lhs = nrm[...].T
        for w, acc in weights:
            rhs = [w[a, zz, xx, start : start + rows, :] for a, zz, xx in spots]
            acc[...] += dot(lhs, jnp.concatenate(rhs, axis=0))

    hand_on(0)

    def chunk(group, carry):
        @pl.when(group < 3)
        def _():
            hand_on(group + 1)

        arrived(0, 2, group)
        project(s.nrm0, 0, group)
        arrived(1, 2, group)
        project(s.nrm1, 1, group)

        @pl.when(group == 0)
        def _():
            ce1.wait_recv()
            s.se2[...] = both_cores(1 - yh, s.pe, s.re1[1 - yh]).astype(BF)
            ce2.start()

        return carry

    lax.fori_loop(0, 4, chunk, 0)

    for t in range(2):
        give = rows_of(t, 1 - core)
        s.sq1[t] = s.pq[give, :].astype(BF)
    cq1 = remote(s.sq1, s.rq1, s.cq.at[0, 0], s.cq.at[1, 0], other_core, gy)
    cq1.start()
    for t in range(2):
        give = rows_of(t, 1 - core)
        s.sg1[t, 0] = s.pg[give, :].astype(BF)
        s.sg1[t, 1] = s.pu[give, :].astype(BF)
    cg1 = remote(s.sg1, s.rg1, s.cg.at[0, 0], s.cg.at[1, 0], other_core, gy)
    cg1.start()
    cq1.wait_recv()

    s.sq2[...] = both_cores(1 - yh, s.pq, s.rq1[1 - yh]).astype(BF)
    cq2 = remote(s.sq2, s.rq2, s.cq.at[0, 1], s.cq.at[1, 1], other_chip, gy)
    cq2.start()
    cg1.wait_recv()
    s.sg2[0] = both_cores(1 - yh, s.pg, s.rg1[1 - yh, 0]).astype(BF)
    s.sg2[1] = both_cores(1 - yh, s.pu, s.rg1[1 - yh, 1]).astype(BF)
    cg2 = remote(s.sg2, s.rg2, s.cg.at[0, 1], s.cg.at[1, 1], other_chip, gy)
    cg2.start()
    ce2.wait_recv()
    entries = both_cores(yh, s.pe, s.re1[yh]) + s.re2[...].astype(F32)
    for k in range(4):
        s.ef[k] = entries[:, 128 * k : 128 * k + 128]
    s.msg[...] = jnp.zeros((512, 128), F32)
    for i in range(2):
        for k in range(4):
            s.msg[pl.ds(6 + 4 * i + k, 32, stride=16), :] = s.ef[k, pl.ds(i, 32, stride=2), :]
    cq2.wait_recv()
    query = both_cores(yh, s.pq, s.rq1[yh]) + s.rq2[...].astype(F32)
    query = query * s.cosq[...] + swap_pairs(query) * s.sinq[...]
    for k in range(3):
        s.qf[k] = query[:, 128 * k : 128 * k + 128]

    for i in range(2):
        for k in range(3):
            s.msg[pl.ds(3 * i + k, 32, stride=16), :] = s.qf[k, pl.ds(i, 32, stride=2), :]
    s.mq[...] = s.msg[...].astype(BF).reshape(32, 16, 128)

    for p in others:
        remote(s.mq.at[p], s.mr.at[gy], s.mqs.at[0], s.mqs.at[1], gx, p).start()
    s.mr[gy] = s.mq[gy]

    cg2.wait_recv()
    gate = both_cores(yh, s.pg, s.rg1[yh, 0]) + s.rg2[0].astype(F32)
    up = both_cores(yh, s.pu, s.rg1[yh, 1]) + s.rg2[1].astype(F32)
    s.hidall[gx] = (gate / (1.0 + jnp.exp(-gate)) * up).astype(BF)
    gather_hidden = [
        remote(
            s.hidall.at[gx], s.hidall.at[gx], s.gh.at[0, d - 1], s.gh.at[1, d - 1], lax.rem(gx + d, 4), gy
        )
        for d in range(1, 4)
    ]
    for cp in gather_hidden:
        cp.start()

    many_q = s.mr.at[pl.ds(0, 31)]
    pltpu.make_async_copy(many_q, many_q, s.mqs.at[1]).wait()
    rest[1].wait()
    rest[2].wait()
    s.msg[...] = s.mr[...].reshape(512, 128).astype(F32)
    scale = 1.0 / math.sqrt(DH)
    first_row = (gx * 32 + gy) * 2
    s.aback[...] = jnp.zeros((32, 8, 128), F32)
    replies = []
    for i in range(2):
        for k in range(3):
            s.pieces[pl.ds(k, 32, stride=3), :] = s.msg[pl.ds(3 * i + k, 32, stride=16), :]
        q = jnp.concatenate(
            [s.pieces[pl.ds(0, 48, stride=2), :], s.pieces[pl.ds(1, 48, stride=2), :]], axis=1
        )
        entry = [
            jnp.sum(s.msg[pl.ds(6 + 4 * i + k, 32, stride=16), :], axis=0, keepdims=True)
            for k in range(4)
        ]
        length = lens[first_row + i]
        key = jnp.broadcast_to(jnp.concatenate(entry[0:2], axis=1), (8, DH))
        value = jnp.concatenate(entry[2:4], axis=1).astype(BF).astype(F32)
        key_cos, key_sin = rope_tables(jnp.full((8, DH), length.astype(F32), F32), 0, (8, DH))
        key = (key * key_cos + swap_pairs(key) * key_sin)[0:1].astype(BF).astype(F32)
        qb = q.astype(BF)
        scores = (
            lax.dot_general(qb, s.keys[i], (((1,), (1,)), ((), ())), preferred_element_type=F32) * scale
        )
        position = lax.broadcasted_iota(jnp.int32, (H, CTX), 1)
        scores = jnp.where(position < length, scores, -1e30)
        own = jnp.sum(q * key, axis=1, keepdims=True) * scale
        peak = jnp.maximum(jnp.max(scores, axis=1, keepdims=True), own)
        expd = jnp.exp(scores - peak)
        own_exp = jnp.exp(own - peak)
        denom = jnp.sum(expd, axis=1, keepdims=True) + own_exp
        weights = (expd / denom).astype(BF)
        own_weight = (own_exp / denom).astype(BF).astype(F32)
        mixed = dot(weights, s.vals[i]) + own_weight * value
        s.pieces[pl.ds(0, 48, stride=2), :] = mixed[:, 0:128]
        s.pieces[pl.ds(1, 48, stride=2), :] = mixed[:, 128:256]
        for k in range(3):
            replies.append((3 * i + k, s.pieces[pl.ds(k, 32, stride=3), :]))
    for row, piece in replies:
        s.msg[pl.ds(row, 32, stride=8), :] = piece
    s.aback[...] = s.msg[0:256, :].reshape(32, 8, 128)

    for p in others:
        remote(s.aback.at[p], s.abackr.at[gy], s.abs_.at[0], s.abs_.at[1], gx, p).start()
    s.abackr[gy] = s.aback[gy]

    for cp in gather_hidden:
        cp.wait_recv()
    rest[3].wait()

    def down(c, carry):
        cols = pl.ds(pl.multiple_of(c * WIDE, 128), WIDE)
        s.outp[:, cols] = dot(s.hidall[...].reshape(ROWS, FC), s.wdv[:, cols])
        return carry

    lax.fori_loop(0, 4, down, 0)

    many_a = s.abackr.at[pl.ds(0, 31)]
    pltpu.make_async_copy(many_a, many_a, s.abs_.at[1]).wait()
    s.msg[0:256, :] = s.abackr[...].reshape(256, 128)
    for i in range(2):
        for k in range(3):
            s.att64[k, pl.ds(i, 32, stride=2), :] = s.msg[pl.ds(3 * i + k, 32, stride=8), :]
    for k in range(3):
        s.attall[gx, :, 128 * k : 128 * k + 128] = s.att64[k].astype(BF)
    gather_att = [
        remote(
            s.attall.at[gx], s.attall.at[gx], s.ga.at[0, d - 1], s.ga.at[1, d - 1], lax.rem(gx + d, 4), gy
        )
        for d in range(1, 4)
    ]
    for cp in gather_att:
        cp.start()
    rest[4].wait()
    for cp in gather_att:
        cp.wait_recv()

    outs = ((s.e0, s.r0, s.y0, s.c0, s.s0), (s.e1, s.r1, s.y1, s.c1, s.s1))

    def block(part, ring_at, dy, dr):
        a = lax.rem(yl + dy, 2)
        r = lax.rem((x, z)[part] + dr, 4)
        start, rows = parts[part]
        where = (a, ring_at, r) if part == 0 else (a, r, ring_at)
        return s.eT.at[(*where, pl.ds(start, rows))]

    def turned_out(half):
        pair = lax.rem(z // 2 + 1 + half, 2)

        def one(a, carry):
            cols = pl.ds(pl.multiple_of((2 * a + pair) * WIDE, 128), WIDE)
            v = s.outp[:, cols] + dot(s.attall[...].reshape(ROWS, QC), s.wov[:, cols])
            s.eT[a, pl.ds(pair * 2, 2)] = v.T.astype(BF).reshape(2, 4, COLS, ROWS)
            return carry

        lax.fori_loop(0, 2, one, 0)

    legs = []

    def leg(part, kind, dy, dr, src, dst, j):
        sem = outs[part][0]
        cp = remote(src, dst, sem.at[0, kind, dy, dr], sem.at[1, kind, dy, dr], gx, ring[1 - part](j))
        cp.start()
        legs.append(cp)
        return cp

    steps = (1, 3)
    ways = (2, 1, 3, 0)
    early = {}

    def send_early(part):
        for dr in ways:
            for dy in range(2):
                early[part, dy, dr] = leg(
                    part, 0, dy, dr, block(part, along(part, 2), dy, dr), outs[part][2].at[dy, dr], steps[dy]
                )

    turned_out(0)
    send_early(0)
    turned_out(1)
    send_early(1)
    plain, joined = {}, {}
    for dr in ways:
        for part in range(2):
            for dy in range(2):
                way = 1 - dy
                plain[part, dy, dr] = leg(
                    part, 1, dy, dr,
                    block(part, along(part, steps[way]), dy, dr), outs[part][1].at[way, dy, dr], steps[way],
                )
    for dr in ways:
        for part in range(2):
            _, got, relay, both, _ = outs[part]
            for dy in range(2):
                early[part, dy, dr].wait_recv()
                mine = block(part, along(part, steps[dy]), dy, dr)
                both[dy, dr] = (mine[...].astype(F32) + relay[dy, dr].astype(F32)).astype(BF)
                joined[part, dy, dr] = leg(
                    part, 2, dy, dr, both.at[dy, dr], got.at[dy, dy, dr], steps[dy]
                )

    last0 = {
        k: remote(s.s0.at[k], s.r0b.at[k], s.f0.at[0, k], s.f0.at[1, k], gx, plane[0](k))
        for k in range(1, 8)
    }
    last1 = {
        k: remote(s.s1.at[k], s.r1b.at[k], s.f1.at[0, k], s.f1.at[1, k], gx, plane[1](k))
        for k in range(1, 8)
    }

    def summed(part, dy, dr):
        plain[part, dy, dr].wait_recv()
        joined[part, dy, dr].wait_recv()
        got = outs[part][1]
        v = block(part, along(part, 0), dy, dr)[...].astype(F32)
        return v + got[0, dy, dr].astype(F32) + got[1, dy, dr].astype(F32)

    order = [4 * dy + dr for dr in ways for dy in (1, 0)][:-1]
    for k in order:
        for part in range(2):
            outs[part][4][k] = summed(part, k // 4, k % 4).astype(BF)
            (last0, last1)[part][k].start()
    v0 = tok[0:PA, :].astype(F32) + summed(0, 0, 0)
    v1 = tok[PA:COLS, :].astype(F32) + summed(1, 0, 0)
    for k in order:
        last0[k].wait_recv()
        v0 = v0 + s.r0b[k].astype(F32)
    out[0:PA, :] = v0
    for k in order:
        last1[k].wait_recv()
        v1 = v1 + s.r1b[k].astype(F32)
    out[PA:COLS, :] = v1

    for group in (
        stat_z, stat_plane, stat_gx, (ce1, ce2, cq1, cg1, cq2, cg2),
        gather_hidden, gather_att, first0.values(), first1.values(), last0.values(), last1.values(),
    ):
        for cp in group:
            cp.wait_send()
    for cp in legs:
        cp.wait_send()
    for part in range(2):
        two = xts[part].at[0, 0, pl.ds(0, 2)]
        for j in range(1, 4):
            for group in range(4):
                pltpu.make_async_copy(two, two, bs[part].at[0, j, group]).wait()
    pltpu.make_async_copy(many_q, many_q, s.mqs.at[0]).wait()
    pltpu.make_async_copy(many_a, many_a, s.abs_.at[0]).wait()


def body(
    tokens, ln_gain, w_query, w_entries, w_out, w_gate, w_up, w_down, cache_keys, cache_values, lengths
):
    vmem = pl.BlockSpec(memory_space=pltpu.VMEM)
    hbm = pl.BlockSpec(memory_space=pl.ANY)
    return pl.pallas_call(
        kernel,
        out_shape=jax.ShapeDtypeStruct((COLS, ROWS), F32),
        in_specs=[vmem, vmem, pl.BlockSpec(memory_space=pltpu.SMEM)] + [hbm] * 8,
        out_specs=vmem,
        scratch_shapes=[pltpu.VMEM(shape, kind) for shape, kind in SCRATCH.values()]
        + [pltpu.SemaphoreType.DMA(shape) for shape in SEMS.values()],
        compiler_params=pltpu.CompilerParams(
            collective_id=0, has_side_effects=True, vmem_limit_bytes=60 << 20
        ),
        name="layer",
    )(
        tokens.T,
        ln_gain.reshape(36, 128),
        lengths,
        w_query.reshape(2, 4, 4, COLS, QC),
        w_gate.T,
        w_up.T,
        w_entries,
        w_out,
        w_down,
        cache_keys,
        cache_values,
    ).T


def solution(mesh):
    return jax.shard_map(
        body,
        mesh=mesh,
        in_specs=(
            P(None, ("gx", "gy")),
            P("gx"),
            P("gx", "gy"),
            P(("gx", "gy"), None),
            P("gy", "gx"),
            P("gx", "gy"),
            P("gx", "gy"),
            P("gy", "gx"),
            P(("gx", "gy"), None, None),
            P(("gx", "gy"), None, None),
            P(None),
        ),
        out_specs=P(None, ("gx", "gy")),
        check_vma=False,
    )
```

```python
import math

import jax
import jax.numpy as jnp
from jax import lax
from jax.experimental import pallas as pl
from jax.experimental.pallas import tpu as pltpu
from jax.sharding import PartitionSpec as P

D = 18432
H = 48
DH = 256
CTX = 1024
EPS = 1e-05
ROWS = 256
COLS = 144
PA, PB = 80, 64
QC = 384
EC = 512
FC = 576
SLAB = 4608
WIDE = 1152
BF = jnp.bfloat16
F32 = jnp.float32
LOG_BASE = -2.0 * math.log(10000.0) / DH


def dot(a, b):
    return jnp.dot(a, b, preferred_element_type=F32)


def remote(src, dst, send, recv, gx, gy):
    return pltpu.make_async_remote_copy(
        src_ref=src,
        dst_ref=dst,
        send_sem=send,
        recv_sem=recv,
        device_id={"gx": gx, "gy": gy},
        device_id_type=pl.DeviceIdType.MESH,
    )


def place(y, z, x):
    return y * 16 + z * 4 + x


def swap_pairs(v):
    width = v.shape[1]
    even = lax.rem(lax.broadcasted_iota(jnp.int32, v.shape, 1), 2) == 0
    return jnp.where(even, pltpu.roll(v, width - 1, 1), pltpu.roll(v, 1, 1))


def rope_tables(positions, offset, shape):
    col = lax.broadcasted_iota(jnp.int32, shape, 1)
    even = lax.rem(col, 2) == 0
    pair = lax.rem(col + offset, DH) // 2
    angle = positions * jnp.exp(pair.astype(F32) * LOG_BASE)
    sine = jnp.sin(angle)
    return jnp.cos(angle), jnp.where(even, -sine, sine)


SCRATCH = dict(
    wqv=((2, 4, 4, COLS, QC), BF),
    wgv=((2, 4, 4, COLS, FC), BF),
    wuv=((2, 4, 4, COLS, FC), BF),
    turn=((8, FC, WIDE), BF),
    wev=((COLS, EC), BF),
    wov=((QC, SLAB), BF),
    wdv=((FC, SLAB), BF),
    keys=((2, CTX, DH), BF),
    vals=((2, CTX, DH), BF),
    gpad=((128, 128), F32),
    gcol=((SLAB, 128), F32),
    xt0=((4, 2, 4, PA, ROWS), BF),
    xt1=((4, 2, 4, PB, ROWS), BF),
    st=((8, 128), F32),
    str_=((3, 8, 128), F32),
    st2=((8, 128), F32),
    st2r=((7, 8, 128), F32),
    st3=((8, 128), F32),
    st3r=((3, 8, 128), F32),
    stat=((8, ROWS), F32),
    nrm0=((8 * PA, ROWS), BF),
    nrm1=((8 * PB, ROWS), BF),
    pq=((ROWS, QC), F32),
    pe=((ROWS, EC), F32),
    pg=((ROWS, FC), F32),
    pu=((ROWS, FC), F32),
    se1=((2, 64, EC), BF),
    re1=((2, 64, EC), BF),
    sq1=((2, 64, QC), BF),
    rq1=((2, 64, QC), BF),
    sg1=((2, 2, 64, FC), BF),
    rg1=((2, 2, 64, FC), BF),
    sg2=((2, 64, FC), BF),
    rg2=((2, 64, FC), BF),
    qf=((2, 3, 64, 128), F32),
    ef=((2, 4, 64, 128), F32),
    msg=((2, 512, 128), F32),
    mq=((64, 16, 128), BF),
    mr=((64, 16, 128), BF),
    pieces=((96, 128), F32),
    aback=((32, 8, 128), F32),
    abackr=((64, 8, 128), F32),
    att64=((2, 3, 64, 128), F32),
    attall=((4, 64, QC), BF),
    hidall=((4, 64, FC), BF),
    outp=((ROWS, SLAB), F32),
    eT=((2, 4, 4, COLS, ROWS), BF),
    r0=((2, 2, 4, PA, ROWS), BF),
    r1=((2, 2, 4, PB, ROWS), BF),
    y0=((2, 4, PA, ROWS), BF),
    y1=((2, 4, PB, ROWS), BF),
    c0=((2, 4, PA, ROWS), BF),
    c1=((2, 4, PB, ROWS), BF),
    s0=((8, PA, ROWS), BF),
    s1=((8, PB, ROWS), BF),
    r0b=((8, PA, ROWS), BF),
    r1b=((8, PB, ROWS), BF),
)
SEMS = dict(
    lw=(9,),
    lx=(5,),
    stg=(2, 3),
    sts=(2, 7),
    stz=(2, 3),
    a0=(2, 8),
    a1=(2, 8),
    b0=(2, 4, 4),
    b1=(2, 4, 4),
    ce=(2,),
    cq=(2,),
    cg=(2, 2),
    mqs=(2,),
    abs_=(2,),
    ga=(2, 2),
    gh=(2, 3),
    e0=(2, 3, 2, 4),
    e1=(2, 3, 2, 4),
    f0=(2, 8),
    f1=(2, 8),
)
NAMES = list(SCRATCH) + list(SEMS)


class Refs:
    pass


def kernel(tok, gain, lens, wq, wgt, wut, we, wo, wd, ck, cv, out, *scratch):
    s = Refs()
    for name, ref in zip(NAMES, scratch):
        setattr(s, name, ref)
    gx = lax.axis_index("gx")
    gy = lax.axis_index("gy")
    yh, core = gx // 2, lax.rem(gx, 2)
    yl, z, x = gy // 16, lax.rem(gy // 4, 4), lax.rem(gy, 4)

    barrier = pltpu.get_barrier_semaphore()

    ring = [lambda d: place(yl, z, lax.rem(x + d, 4)), lambda d: place(yl, lax.rem(z + d, 4), x)]
    plane = [
        lambda k: place(lax.rem(yl + k // 4, 2), z, lax.rem(x + k % 4, 4)),
        lambda k: place(lax.rem(yl + k // 4, 2), lax.rem(z + k % 4, 4), x),
    ]
    far = (2, 1, 3, 0)
    others = [
        place(lax.rem(yl + dy, 2), lax.rem(z + dz, 4), lax.rem(x + dx, 4))
        for dy in (1, 0)
        for dz in far
        for dx in far
    ][:-1]
    greeted = [(lax.rem(gx + d, 4), gy) for d in range(1, 4)]
    greeted += [(gx, plane[0](k)) for k in range(1, 8)]
    greeted += [(gx, plane[1](k)) for k in (1, 2, 3, 5, 6, 7)]
    for to_x, to_y in greeted:
        pl.semaphore_signal(
            barrier, inc=1, device_id={"gx": to_x, "gy": to_y}, device_id_type=pl.DeviceIdType.MESH
        )
    loads = []
    for c in range(8):
        src = (wgt, wut)[c // 4].at[:, pl.ds(WIDE * (c % 4), WIDE)]
        loads.append(pltpu.make_async_copy(src, s.turn.at[c], s.lw.at[c]))
    loads.append(pltpu.make_async_copy(wq, s.wqv, s.lw.at[8]))
    rest = [
        pltpu.make_async_copy(a, b, s.lx.at[k])
        for k, (a, b) in enumerate(
            ((we, s.wev), (ck, s.keys), (cv, s.vals), (wd, s.wdv), (wo, s.wov))
        )
    ]
    for cp in loads[:8]:
        cp.start()

    own0 = s.xt0.at[z, yl, x]
    own1 = s.xt1.at[x, yl, z]
    own0[...] = tok[0:PA, :]
    own1[...] = tok[PA:COLS, :]
    columns = tok[...].astype(F32)
    total = jnp.sum(columns, axis=0, keepdims=True)
    squares = jnp.sum(columns * columns, axis=0, keepdims=True)
    s.st[...] = jnp.zeros((8, 128), F32)
    s.st[0:1, :] = total[:, 0:128]
    s.st[1:2, :] = total[:, 128:256]
    s.st[2:3, :] = squares[:, 0:128]
    s.st[3:4, :] = squares[:, 128:256]

    def turn_weights(m, dst):
        def one(c, carry):
            at = m * 4 + c
            pltpu.make_async_copy(s.turn.at[at], s.turn.at[at], s.lw.at[at]).wait()
            dst[c // 2, pl.ds(lax.rem(c, 2) * 2, 2)] = s.turn[at].T.reshape(2, 4, COLS, FC)
            return carry

        lax.fori_loop(0, 4, one, 0)

    s.gpad[...] = jnp.zeros((128, 128), F32)
    s.gpad[0:36, :] = gain[...]
    gain_turned = s.gpad[...].T
    for c in range(36):
        s.gcol[128 * c : 128 * c + 128, :] = jnp.broadcast_to(gain_turned[:, c : c + 1], (128, 128))

    s.pq[...] = jnp.zeros((ROWS, QC), F32)
    s.pg[...] = jnp.zeros((ROWS, FC), F32)
    s.pu[...] = jnp.zeros((ROWS, FC), F32)
    pl.semaphore_wait(barrier, len(greeted))

    stat_plane = [
        remote(s.st, s.st2r.at[k - 1], s.sts.at[0, k - 1], s.sts.at[1, k - 1], gx, plane[0](k))
        for k in range(1, 8)
    ]
    for cp in stat_plane:
        cp.start()
    order = (4, 1, 3, 5, 2, 7, 6)
    first0 = {
        k: remote(own0, own0, s.a0.at[0, k], s.a0.at[1, k], gx, plane[0](k)) for k in order
    }
    first1 = {
        k: remote(own1, own1, s.a1.at[0, k], s.a1.at[1, k], gx, plane[1](k)) for k in order
    }
    for k in order:
        first0[k].start()
        first1[k].start()
    for cp in loads[8:] + rest:
        cp.start()

    xts, bs, parts = (s.xt0, s.xt1), (s.b0, s.b1), ((0, PA), (PA, PB))

    def shard(part, ring_at, dy, dr):
        a = lax.rem(yl + dy, 2)
        return xts[part].at[ring_at, a, lax.rem((x, z)[part] + 4 - dr, 4)]

    def along(part, d):
        return lax.rem((z, x)[part] + d, 4)

    def forward(k):
        group = (0, 1, 3, 2)[k % 4]
        for part in range(2):
            if k > 0:
                (first0, first1)[part][k].wait_recv()
            piece = shard(part, along(part, 0), k // 4, k % 4)
            for j in (1, 3):
                remote(
                    piece, piece, bs[part].at[0, j, group], bs[part].at[1, j, group], gx, ring[1 - part](j)
                ).start()

    def arrived(part, j, group):
        two = xts[part].at[0, 0, pl.ds(0, 2)]
        pltpu.make_async_copy(two, two, bs[part].at[1, j, group]).wait()

    def hand_on(group):
        dr = group + group // 2 - 2 * (group // 3)
        for part in range(2):
            for j, back, dy in ((1, 3, 0), (3, 1, 1)):
                arrived(part, j, group)
                piece = shard(part, along(part, back), dy, dr)
                remote(
                    piece, piece, bs[part].at[0, 2, group], bs[part].at[1, 2, group], gx, ring[1 - part](j)
                ).start()

    forward(0)
    turn_weights(1, s.wuv)
    for cp in stat_plane:
        cp.wait_recv()
    s.st2[...] = s.st[...] + jnp.sum(s.st2r[...], axis=0)
    stat_z = [
        remote(s.st2, s.str_.at[j - 1], s.stg.at[0, j - 1], s.stg.at[1, j - 1], gx, ring[1](j))
        for j in range(1, 4)
    ]
    for cp in stat_z:
        cp.start()
    for k in (4, 1, 3, 2):
        forward(k)
    turn_weights(0, s.wgv)
    forward(5)
    for cp in stat_z:
        cp.wait_recv()
    s.st3[...] = s.st2[...] + s.str_[0] + s.str_[1] + s.str_[2]
    stat_gx = [
        remote(s.st3, s.st3r.at[d - 1], s.stz.at[0, d - 1], s.stz.at[1, d - 1], lax.rem(gx + d, 4), gy)
        for d in range(1, 4)
    ]
    for cp in stat_gx:
        cp.start()
    for k in (7, 6):
        forward(k)
    hand_on(0)

    for cp in stat_gx:
        cp.wait_recv()
    sums = (s.st3[...] + jnp.sum(s.st3r[...], axis=0)) * (1.0 / D)
    average = jnp.concatenate([sums[0:1], sums[1:2]], axis=1)
    meansq = jnp.concatenate([sums[2:3], sums[3:4]], axis=1)
    s.stat[0:1, :] = average
    s.stat[1:2, :] = lax.rsqrt(meansq - average * average + EPS)

    def normalize(block, start, rows):
        g = s.gcol[pl.ds(pl.multiple_of(start, 16), rows), :]
        g = jnp.concatenate([g, g], axis=1)
        return ((block.astype(F32) - s.stat[0:1, :]) * s.stat[1:2, :] * g).astype(BF)

    local = normalize(tok[...], gy * COLS, COLS)
    rest[0].wait()
    s.pe[...] = dot(local.T, s.wev[...])

    def rows_of(t, c):
        return pl.ds(pl.multiple_of((2 * t + c) * 64, 64), 64)

    def both_cores(t, acc, got):
        return acc[rows_of(t, core), :] + got.astype(F32)

    other_core = yh * 2 + 1 - core
    other_chip = (1 - yh) * 2 + core
    for t in range(2):
        s.se1[t] = s.pe[rows_of(t, 1 - core), :].astype(BF)
    ce1 = remote(s.se1, s.re1, s.ce.at[0], s.ce.at[1], other_core, gy)
    ce1.start()

    weights = ((s.wqv, s.pq), (s.wgv, s.pg), (s.wuv, s.pu))
    loads[8].wait()

    def prepare(nrm, part, pieces):
        start, rows = parts[part]
        spots = []
        for ring_at, dy, dr in pieces:
            a = lax.rem(yl + dy, 2)
            r = lax.rem((x, z)[part] + 4 - dr, 4)
            spots.append((a, ring_at, r) if part == 0 else (a, r, ring_at))
        for i, (a, zz, xx) in enumerate(spots):
            block = s.xt0[zz, a, xx] if part == 0 else s.xt1[xx, a, zz]
            nrm[i * rows : (i + 1) * rows, :] = normalize(block, place(a, zz, xx) * COLS + start, rows)
        return nrm[0 : len(spots) * rows, :].T, spots

    def project(part, lhs, spots, only):
        start, rows = parts[part]
        for w, acc in only:
            rhs = [w[a, zz, xx, start : start + rows, :] for a, zz, xx in spots]
            acc[...] += dot(lhs, jnp.concatenate(rhs, axis=0))

    def chunk(group, carry):
        @pl.when(group > 0)
        def _():
            hand_on(group)

        dr = group + group // 2 - 2 * (group // 3)
        for part in range(2):
            near = [(along(part, d), dy, dr) for dy in range(2) for d in (0, 1, 3)]
            project(part, *prepare((s.nrm0, s.nrm1)[part], part, near), weights)

        return carry

    lax.fori_loop(0, 4, chunk, 0)
    ready = []
    for part in range(2):
        for group in range(4):
            arrived(part, 2, group)
        distant = [(along(part, 2), dy, dr) for dy in range(2) for dr in range(4)]
        ready.append((part, *prepare((s.nrm0, s.nrm1)[part], part, distant)))
        project(*ready[part], weights[:1])

    for t in range(2):
        s.sq1[t] = s.pq[rows_of(t, 1 - core), :].astype(BF)
    cq1 = remote(s.sq1, s.rq1, s.cq.at[0], s.cq.at[1], other_core, gy)
    cq1.start()
    ce1.wait_recv()
    for t in range(2):
        entries = both_cores(t, s.pe, s.re1[t])
        s.msg[t] = jnp.zeros((512, 128), F32)
        for k in range(4):
            s.ef[t, k] = entries[:, 128 * k : 128 * k + 128]
            for i in range(2):
                s.msg[t, pl.ds(6 + 4 * i + k, 32, stride=16), :] = s.ef[t, k, pl.ds(i, 32, stride=2), :]
    cq1.wait_recv()

    for t in range(2):
        query = both_cores(t, s.pq, s.rq1[t])
        for k in range(3):
            s.qf[t, k] = query[:, 128 * k : 128 * k + 128]
            for i in range(2):
                s.msg[t, pl.ds(3 * i + k, 32, stride=16), :] = s.qf[t, k, pl.ds(i, 32, stride=2), :]
    s.mq[...] = s.msg[...].astype(BF).reshape(64, 16, 128)
    own_slot = yh * 32 + gy
    partners = [(1 - yh, p) for p in others + [gy]] + [(yh, p) for p in others]
    for to, p in partners:
        remote(
            s.mq.at[to * 32 + p], s.mr.at[own_slot], s.mqs.at[0], s.mqs.at[1], to * 2 + core, p
        ).start()
    s.mr[own_slot] = s.mq[own_slot]

    for item in ready:
        project(*item, weights[1:])
    for t in range(2):
        give = rows_of(t, 1 - core)
        s.sg1[t, 0] = s.pg[give, :].astype(BF)
        s.sg1[t, 1] = s.pu[give, :].astype(BF)
    cg1 = remote(s.sg1, s.rg1, s.cg.at[0, 0], s.cg.at[1, 0], other_core, gy)
    cg1.start()
    cg1.wait_recv()
    s.sg2[0] = both_cores(1 - yh, s.pg, s.rg1[1 - yh, 0]).astype(BF)
    s.sg2[1] = both_cores(1 - yh, s.pu, s.rg1[1 - yh, 1]).astype(BF)
    cg2 = remote(s.sg2, s.rg2, s.cg.at[0, 1], s.cg.at[1, 1], other_chip, gy)
    cg2.start()

    first_row = (gx * 32 + gy) * 2
    turns = []
    for i in range(2):
        at = jnp.full((8, DH), lens[first_row + i].astype(F32), F32)
        turns.append([v[0:1] for v in rope_tables(at, 0, (8, DH))])

    cg2.wait_recv()
    gate = both_cores(yh, s.pg, s.rg1[yh, 0]) + s.rg2[0].astype(F32)
    up = both_cores(yh, s.pu, s.rg1[yh, 1]) + s.rg2[1].astype(F32)
    s.hidall[gx] = (gate / (1.0 + jnp.exp(-gate)) * up).astype(BF)
    gather_hidden = [
        remote(
            s.hidall.at[gx], s.hidall.at[gx], s.gh.at[0, d - 1], s.gh.at[1, d - 1], lax.rem(gx + d, 4), gy
        )
        for d in range(1, 4)
    ]
    for cp in gather_hidden:
        cp.start()

    many_q = s.mr.at[pl.ds(0, 63)]
    pltpu.make_async_copy(many_q, many_q, s.mqs.at[1]).wait()
    rest[1].wait()
    rest[2].wait()
    s.msg[...] = s.mr[...].reshape(2, 512, 128).astype(F32)
    s.msg[0] = s.msg[0] + s.msg[1]
    scale = 1.0 / math.sqrt(DH)
    s.aback[...] = jnp.zeros((32, 8, 128), F32)
    replies = []
    for i in range(2):
        for k in range(3):
            s.pieces[pl.ds(k, 32, stride=3), :] = s.msg[0, pl.ds(3 * i + k, 32, stride=16), :]
        q = jnp.concatenate(
            [s.pieces[pl.ds(0, 48, stride=2), :], s.pieces[pl.ds(1, 48, stride=2), :]], axis=1
        )
        cosine, sine = turns[i]
        q = q * cosine + swap_pairs(q) * sine
        qb = q.astype(BF)
        entry = [
            jnp.sum(s.msg[0, pl.ds(6 + 4 * i + k, 32, stride=16), :], axis=0, keepdims=True)
            for k in range(4)
        ]
        length = lens[first_row + i]
        key = jnp.broadcast_to(jnp.concatenate(entry[0:2], axis=1), (8, DH))
        value = jnp.concatenate(entry[2:4], axis=1).astype(BF).astype(F32)
        key = (key * cosine + swap_pairs(key) * sine)[0:1].astype(BF).astype(F32)
        scores = (
            lax.dot_general(qb, s.keys[i], (((1,), (1,)), ((), ())), preferred_element_type=F32) * scale
        )
        position = lax.broadcasted_iota(jnp.int32, (H, CTX), 1)
        scores = jnp.where(position < length, scores, -1e30)
        own = jnp.sum(qb.astype(F32) * key, axis=1, keepdims=True) * scale
        peak = jnp.maximum(jnp.max(scores, axis=1, keepdims=True), own)
        expd = jnp.exp(scores - peak)
        own_exp = jnp.exp(own - peak)
        denom = jnp.sum(expd, axis=1, keepdims=True) + own_exp
        weights = (expd / denom).astype(BF)
        own_weight = (own_exp / denom).astype(BF).astype(F32)
        mixed = dot(weights, s.vals[i]) + own_weight * value
        s.pieces[pl.ds(0, 48, stride=2), :] = mixed[:, 0:128]
        s.pieces[pl.ds(1, 48, stride=2), :] = mixed[:, 128:256]
        for k in range(3):
            replies.append((3 * i + k, s.pieces[pl.ds(k, 32, stride=3), :]))
    for row, piece in replies:
        s.msg[0, pl.ds(row, 32, stride=8), :] = piece
    s.aback[...] = s.msg[0, 0:256, :].reshape(32, 8, 128)

    for to, p in partners:
        remote(
            s.aback.at[p], s.abackr.at[own_slot], s.abs_.at[0], s.abs_.at[1], to * 2 + core, p
        ).start()
    s.abackr[own_slot] = s.aback[gy]

    for cp in gather_hidden:
        cp.wait_recv()
    rest[3].wait()

    def down(c, carry):
        cols = pl.ds(pl.multiple_of(c * WIDE, 128), WIDE)
        s.outp[:, cols] = dot(s.hidall[...].reshape(ROWS, FC), s.wdv[:, cols])
        return carry

    lax.fori_loop(0, 4, down, 0)

    many_a = s.abackr.at[pl.ds(0, 63)]
    pltpu.make_async_copy(many_a, many_a, s.abs_.at[1]).wait()
    s.msg[0] = s.abackr[...].reshape(512, 128)
    gather_att = []
    for t in range(2):
        at = 2 * t + core
        for k in range(3):
            for i in range(2):
                s.att64[t, k, pl.ds(i, 32, stride=2), :] = s.msg[
                    0, pl.ds(256 * t + 3 * i + k, 32, stride=8), :
                ]
            s.attall[at, :, 128 * k : 128 * k + 128] = s.att64[t, k].astype(BF)
        gather_att.append(
            remote(s.attall.at[at], s.attall.at[at], s.ga.at[0, t], s.ga.at[1, t], other_core, gy)
        )
        gather_att[t].start()
    rest[4].wait()
    for cp in gather_att:
        cp.wait_recv()

    outs = ((s.e0, s.r0, s.y0, s.c0, s.s0), (s.e1, s.r1, s.y1, s.c1, s.s1))

    def block(part, ring_at, dy, dr):
        a = lax.rem(yl + dy, 2)
        r = lax.rem((x, z)[part] + dr, 4)
        start, rows = parts[part]
        where = (a, ring_at, r) if part == 0 else (a, r, ring_at)
        return s.eT.at[(*where, pl.ds(start, rows))]

    def turned_out(half):
        pair = lax.rem(z // 2 + 1 + half, 2)

        def one(a, carry):
            cols = pl.ds(pl.multiple_of((2 * a + pair) * WIDE, 128), WIDE)
            v = s.outp[:, cols] + dot(s.attall[...].reshape(ROWS, QC), s.wov[:, cols])
            s.eT[a, pl.ds(pair * 2, 2)] = v.T.astype(BF).reshape(2, 4, COLS, ROWS)
            return carry

        lax.fori_loop(0, 2, one, 0)

    legs = []

    def leg(part, kind, dy, dr, src, dst, j):
        sem = outs[part][0]
        cp = remote(src, dst, sem.at[0, kind, dy, dr], sem.at[1, kind, dy, dr], gx, ring[1 - part](j))
        cp.start()
        legs.append(cp)
        return cp

    steps = (1, 3)
    ways = (2, 1, 3, 0)
    early = {}

    def send_early(part):
        for dr in ways:
            for dy in range(2):
                early[part, dy, dr] = leg(
                    part, 0, dy, dr, block(part, along(part, 2), dy, dr), outs[part][2].at[dy, dr], steps[dy]
                )

    turned_out(0)
    send_early(0)
    turned_out(1)
    send_early(1)
    plain, joined = {}, {}
    for dr in ways:
        for part in range(2):
            for dy in range(2):
                way = 1 - dy
                plain[part, dy, dr] = leg(
                    part, 1, dy, dr,
                    block(part, along(part, steps[way]), dy, dr), outs[part][1].at[way, dy, dr], steps[way],
                )
    for dr in ways:
        for part in range(2):
            _, got, relay, both, _ = outs[part]
            for dy in range(2):
                early[part, dy, dr].wait_recv()
                mine = block(part, along(part, steps[dy]), dy, dr)
                both[dy, dr] = (mine[...].astype(F32) + relay[dy, dr].astype(F32)).astype(BF)
                joined[part, dy, dr] = leg(
                    part, 2, dy, dr, both.at[dy, dr], got.at[dy, dy, dr], steps[dy]
                )

    last0 = {
        k: remote(s.s0.at[k], s.r0b.at[k], s.f0.at[0, k], s.f0.at[1, k], gx, plane[0](k))
        for k in range(1, 8)
    }
    last1 = {
        k: remote(s.s1.at[k], s.r1b.at[k], s.f1.at[0, k], s.f1.at[1, k], gx, plane[1](k))
        for k in range(1, 8)
    }

    def summed(part, dy, dr):
        plain[part, dy, dr].wait_recv()
        joined[part, dy, dr].wait_recv()
        got = outs[part][1]
        v = block(part, along(part, 0), dy, dr)[...].astype(F32)
        return v + got[0, dy, dr].astype(F32) + got[1, dy, dr].astype(F32)

    order = [4 * dy + dr for dr in ways for dy in (1, 0)][:-1]
    for k in order:
        for part in range(2):
            outs[part][4][k] = summed(part, k // 4, k % 4).astype(BF)
            (last0, last1)[part][k].start()
    v0 = tok[0:PA, :].astype(F32) + summed(0, 0, 0)
    v1 = tok[PA:COLS, :].astype(F32) + summed(1, 0, 0)
    for k in order:
        last0[k].wait_recv()
        v0 = v0 + s.r0b[k].astype(F32)
    out[0:PA, :] = v0
    for k in order:
        last1[k].wait_recv()
        v1 = v1 + s.r1b[k].astype(F32)
    out[PA:COLS, :] = v1

    for group in (
        stat_z, stat_plane, stat_gx, (ce1, cq1, cg1, cg2),
        gather_hidden, gather_att, first0.values(), first1.values(), last0.values(), last1.values(),
    ):
        for cp in group:
            cp.wait_send()
    for cp in legs:
        cp.wait_send()
    for part in range(2):
        two = xts[part].at[0, 0, pl.ds(0, 2)]
        for j in range(1, 4):
            for group in range(4):
                pltpu.make_async_copy(two, two, bs[part].at[0, j, group]).wait()
    pltpu.make_async_copy(many_q, many_q, s.mqs.at[0]).wait()
    pltpu.make_async_copy(many_a, many_a, s.abs_.at[0]).wait()


def body(
    tokens, ln_gain, w_query, w_entries, w_out, w_gate, w_up, w_down, cache_keys, cache_values, lengths
):
    vmem = pl.BlockSpec(memory_space=pltpu.VMEM)
    hbm = pl.BlockSpec(memory_space=pl.ANY)
    return pl.pallas_call(
        kernel,
        out_shape=jax.ShapeDtypeStruct((COLS, ROWS), F32),
        in_specs=[vmem, vmem, pl.BlockSpec(memory_space=pltpu.SMEM)] + [hbm] * 8,
        out_specs=vmem,
        scratch_shapes=[pltpu.VMEM(shape, kind) for shape, kind in SCRATCH.values()]
        + [pltpu.SemaphoreType.DMA(shape) for shape in SEMS.values()],
        compiler_params=pltpu.CompilerParams(
            collective_id=0, has_side_effects=True, vmem_limit_bytes=60 << 20
        ),
        name="layer",
    )(
        tokens.T,
        ln_gain.reshape(36, 128),
        lengths,
        w_query.reshape(2, 4, 4, COLS, QC),
        w_gate.T,
        w_up.T,
        w_entries,
        w_out,
        w_down,
        cache_keys,
        cache_values,
    ).T


def solution(mesh):
    return jax.shard_map(
        body,
        mesh=mesh,
        in_specs=(
            P(None, ("gx", "gy")),
            P("gx"),
            P("gx", "gy"),
            P(("gx", "gy"), None),
            P("gy", "gx"),
            P("gx", "gy"),
            P("gx", "gy"),
            P("gy", "gx"),
            P(("gx", "gy"), None, None),
            P(("gx", "gy"), None, None),
            P(None),
        ),
        out_specs=P(None, ("gx", "gy")),
        check_vma=False,
    )
```

```python
import math

import jax
import jax.numpy as jnp
from jax import lax
from jax.experimental import pallas as pl
from jax.experimental.pallas import tpu as pltpu
from jax.sharding import PartitionSpec as P

D = 18432
H = 48
DH = 256
CTX = 1024
EPS = 1e-05
ROWS = 256
COLS = 144
PA, PB = 80, 64
QC = 384
EC = 512
FC = 576
SLAB = 4608
WIDE = 1152
BF = jnp.bfloat16
F32 = jnp.float32
LOG_BASE = -2.0 * math.log(10000.0) / DH


def dot(a, b):
    return jnp.dot(a, b, preferred_element_type=F32)


def remote(src, dst, send, recv, gx, gy):
    return pltpu.make_async_remote_copy(
        src_ref=src,
        dst_ref=dst,
        send_sem=send,
        recv_sem=recv,
        device_id={"gx": gx, "gy": gy},
        device_id_type=pl.DeviceIdType.MESH,
    )


def place(y, z, x):
    return y * 16 + z * 4 + x


def swap_pairs(v):
    width = v.shape[1]
    even = lax.rem(lax.broadcasted_iota(jnp.int32, v.shape, 1), 2) == 0
    return jnp.where(even, pltpu.roll(v, width - 1, 1), pltpu.roll(v, 1, 1))


def rope_tables(positions, offset, shape):
    col = lax.broadcasted_iota(jnp.int32, shape, 1)
    even = lax.rem(col, 2) == 0
    pair = lax.rem(col + offset, DH) // 2
    angle = positions * jnp.exp(pair.astype(F32) * LOG_BASE)
    sine = jnp.sin(angle)
    return jnp.cos(angle), jnp.where(even, -sine, sine)


SCRATCH = dict(
    wqv=((2, 4, 4, COLS, QC), BF),
    wgv=((2, 4, 4, COLS, FC), BF),
    wuv=((2, 4, 4, COLS, FC), BF),
    turn=((8, FC, WIDE), BF),
    wev=((COLS, EC), BF),
    wov=((QC, SLAB), BF),
    wdv=((FC, SLAB), BF),
    keys=((2, CTX, DH), BF),
    vals=((2, CTX, DH), BF),
    gpad=((128, 128), F32),
    gcol=((SLAB, 128), F32),
    xt0=((4, 2, 4, PA, ROWS), BF),
    xt1=((4, 2, 4, PB, ROWS), BF),
    st=((8, 128), F32),
    str_=((3, 8, 128), F32),
    st2=((8, 128), F32),
    st2r=((7, 8, 128), F32),
    st3=((8, 128), F32),
    st3r=((3, 8, 128), F32),
    stat=((8, ROWS), F32),
    nrm0=((8 * PA, ROWS), BF),
    nrm1=((8 * PB, ROWS), BF),
    pq=((ROWS, QC), F32),
    pe=((ROWS, EC), F32),
    pg=((ROWS, FC), F32),
    pu=((ROWS, FC), F32),
    se1=((2, 64, EC), BF),
    re1=((2, 64, EC), BF),
    sq1=((2, 64, QC), BF),
    rq1=((2, 64, QC), BF),
    sg1=((2, 2, 64, FC), BF),
    rg1=((2, 2, 64, FC), BF),
    sg2=((2, 64, FC), BF),
    rg2=((2, 64, FC), BF),
    qf=((2, 3, 64, 128), F32),
    ef=((2, 4, 64, 128), F32),
    msg=((2, 512, 128), F32),
    mq=((64, 16, 128), BF),
    mr=((64, 16, 128), BF),
    pieces=((96, 128), F32),
    aback=((32, 8, 128), F32),
    abackr=((64, 8, 128), F32),
    att64=((2, 3, 64, 128), F32),
    attall=((4, 64, QC), BF),
    hidall=((4, 64, FC), BF),
    outp=((2, ROWS, WIDE), F32),
    eT=((2, 4, 4, COLS, ROWS), BF),
    r0=((2, 2, 4, PA, ROWS), BF),
    r1=((2, 2, 4, PB, ROWS), BF),
    y0=((2, 4, PA, ROWS), BF),
    y1=((2, 4, PB, ROWS), BF),
    c0=((2, 4, PA, ROWS), BF),
    c1=((2, 4, PB, ROWS), BF),
    s0=((8, PA, ROWS), BF),
    s1=((8, PB, ROWS), BF),
    r0b=((8, PA, ROWS), BF),
    r1b=((8, PB, ROWS), BF),
)
SEMS = dict(
    lw=(9,),
    lx=(5,),
    stg=(2, 3),
    sts=(2, 7),
    stz=(2, 3),
    a0=(2, 8),
    a1=(2, 8),
    b0=(2, 4, 4),
    b1=(2, 4, 4),
    ce=(2,),
    cq=(2,),
    cg=(2, 2),
    mqs=(2,),
    abs_=(2,),
    ga=(2, 2),
    gh=(2, 3),
    e0=(2, 3, 2, 4),
    e1=(2, 3, 2, 4),
    f0=(2, 8),
    f1=(2, 8),
)
NAMES = list(SCRATCH) + list(SEMS)


class Refs:
    pass


def kernel(tok, gain, lens, wq, wgt, wut, we, wo, wd, ck, cv, out, *scratch):
    s = Refs()
    for name, ref in zip(NAMES, scratch):
        setattr(s, name, ref)
    gx = lax.axis_index("gx")
    gy = lax.axis_index("gy")
    yh, core = gx // 2, lax.rem(gx, 2)
    yl, z, x = gy // 16, lax.rem(gy // 4, 4), lax.rem(gy, 4)

    barrier = pltpu.get_barrier_semaphore()

    ring = [lambda d: place(yl, z, lax.rem(x + d, 4)), lambda d: place(yl, lax.rem(z + d, 4), x)]
    plane = [
        lambda k: place(lax.rem(yl + k // 4, 2), z, lax.rem(x + k % 4, 4)),
        lambda k: place(lax.rem(yl + k // 4, 2), lax.rem(z + k % 4, 4), x),
    ]
    far = (2, 1, 3, 0)
    others = [
        place(lax.rem(yl + dy, 2), lax.rem(z + dz, 4), lax.rem(x + dx, 4))
        for dy in (1, 0)
        for dz in far
        for dx in far
    ][:-1]
    greeted = [(lax.rem(gx + d, 4), gy) for d in range(1, 4)]
    greeted += [(gx, plane[0](k)) for k in range(1, 8)]
    greeted += [(gx, plane[1](k)) for k in (1, 2, 3, 5, 6, 7)]
    for to_x, to_y in greeted:
        pl.semaphore_signal(
            barrier, inc=1, device_id={"gx": to_x, "gy": to_y}, device_id_type=pl.DeviceIdType.MESH
        )
    loads = []
    for c in range(8):
        src = (wgt, wut)[c // 4].at[:, pl.ds(WIDE * (c % 4), WIDE)]
        loads.append(pltpu.make_async_copy(src, s.turn.at[c], s.lw.at[c]))
    loads.append(pltpu.make_async_copy(wq, s.wqv, s.lw.at[8]))
    rest = [
        pltpu.make_async_copy(a, b, s.lx.at[k])
        for k, (a, b) in enumerate(
            ((we, s.wev), (ck, s.keys), (cv, s.vals), (wd, s.wdv), (wo, s.wov))
        )
    ]
    for cp in loads[:8]:
        cp.start()

    own0 = s.xt0.at[z, yl, x]
    own1 = s.xt1.at[x, yl, z]
    own0[...] = tok[0:PA, :]
    own1[...] = tok[PA:COLS, :]
    columns = tok[...].astype(F32)
    total = jnp.sum(columns, axis=0, keepdims=True)
    squares = jnp.sum(columns * columns, axis=0, keepdims=True)
    s.st[...] = jnp.zeros((8, 128), F32)
    s.st[0:1, :] = total[:, 0:128]
    s.st[1:2, :] = total[:, 128:256]
    s.st[2:3, :] = squares[:, 0:128]
    s.st[3:4, :] = squares[:, 128:256]

    def turn_weights(m, dst):
        def one(c, carry):
            at = m * 4 + c
            pltpu.make_async_copy(s.turn.at[at], s.turn.at[at], s.lw.at[at]).wait()
            dst[c // 2, pl.ds(lax.rem(c, 2) * 2, 2)] = s.turn[at].T.reshape(2, 4, COLS, FC)
            return carry

        lax.fori_loop(0, 4, one, 0)

    s.gpad[...] = jnp.zeros((128, 128), F32)
    s.gpad[0:36, :] = gain[...]
    gain_turned = s.gpad[...].T
    for c in range(36):
        s.gcol[128 * c : 128 * c + 128, :] = jnp.broadcast_to(gain_turned[:, c : c + 1], (128, 128))

    s.pq[...] = jnp.zeros((ROWS, QC), F32)
    s.pg[...] = jnp.zeros((ROWS, FC), F32)
    s.pu[...] = jnp.zeros((ROWS, FC), F32)
    pl.semaphore_wait(barrier, len(greeted))

    stat_plane = [
        remote(s.st, s.st2r.at[k - 1], s.sts.at[0, k - 1], s.sts.at[1, k - 1], gx, plane[0](k))
        for k in range(1, 8)
    ]
    for cp in stat_plane:
        cp.start()
    order = (4, 1, 3, 5, 2, 7, 6)
    first0 = {
        k: remote(own0, own0, s.a0.at[0, k], s.a0.at[1, k], gx, plane[0](k)) for k in order
    }
    first1 = {
        k: remote(own1, own1, s.a1.at[0, k], s.a1.at[1, k], gx, plane[1](k)) for k in order
    }
    for k in order:
        first0[k].start()
        first1[k].start()
    for cp in loads[8:] + rest:
        cp.start()

    xts, bs, parts = (s.xt0, s.xt1), (s.b0, s.b1), ((0, PA), (PA, PB))

    def shard(part, ring_at, dy, dr):
        a = lax.rem(yl + dy, 2)
        return xts[part].at[ring_at, a, lax.rem((x, z)[part] + 4 - dr, 4)]

    def along(part, d):
        return lax.rem((z, x)[part] + d, 4)

    def forward(k):
        group = (0, 1, 3, 2)[k % 4]
        for part in range(2):
            if k > 0:
                (first0, first1)[part][k].wait_recv()
            piece = shard(part, along(part, 0), k // 4, k % 4)
            for j in (1, 3):
                remote(
                    piece, piece, bs[part].at[0, j, group], bs[part].at[1, j, group], gx, ring[1 - part](j)
                ).start()

    def arrived(part, j, group):
        two = xts[part].at[0, 0, pl.ds(0, 2)]
        pltpu.make_async_copy(two, two, bs[part].at[1, j, group]).wait()

    def hand_on(group):
        dr = group + group // 2 - 2 * (group // 3)
        for part in range(2):
            for j, back, dy in ((1, 3, 0), (3, 1, 1)):
                arrived(part, j, group)
                piece = shard(part, along(part, back), dy, dr)
                remote(
                    piece, piece, bs[part].at[0, 2, group], bs[part].at[1, 2, group], gx, ring[1 - part](j)
                ).start()

    forward(0)
    turn_weights(1, s.wuv)
    for cp in stat_plane:
        cp.wait_recv()
    s.st2[...] = s.st[...] + jnp.sum(s.st2r[...], axis=0)
    stat_z = [
        remote(s.st2, s.str_.at[j - 1], s.stg.at[0, j - 1], s.stg.at[1, j - 1], gx, ring[1](j))
        for j in range(1, 4)
    ]
    for cp in stat_z:
        cp.start()
    for k in (4, 1, 3, 2):
        forward(k)
    turn_weights(0, s.wgv)
    forward(5)
    for cp in stat_z:
        cp.wait_recv()
    s.st3[...] = s.st2[...] + s.str_[0] + s.str_[1] + s.str_[2]
    stat_gx = [
        remote(s.st3, s.st3r.at[d - 1], s.stz.at[0, d - 1], s.stz.at[1, d - 1], lax.rem(gx + d, 4), gy)
        for d in range(1, 4)
    ]
    for cp in stat_gx:
        cp.start()
    for k in (7, 6):
        forward(k)
    hand_on(0)

    for cp in stat_gx:
        cp.wait_recv()
    sums = (s.st3[...] + jnp.sum(s.st3r[...], axis=0)) * (1.0 / D)
    average = jnp.concatenate([sums[0:1], sums[1:2]], axis=1)
    meansq = jnp.concatenate([sums[2:3], sums[3:4]], axis=1)
    s.stat[0:1, :] = average
    s.stat[1:2, :] = lax.rsqrt(meansq - average * average + EPS)

    def normalize(block, start, rows):
        g = s.gcol[pl.ds(pl.multiple_of(start, 16), rows), :]
        g = jnp.concatenate([g, g], axis=1)
        return ((block.astype(F32) - s.stat[0:1, :]) * s.stat[1:2, :] * g).astype(BF)

    local = normalize(tok[...], gy * COLS, COLS)
    rest[0].wait()
    s.pe[...] = dot(local.T, s.wev[...])

    def rows_of(t, c):
        return pl.ds(pl.multiple_of((2 * t + c) * 64, 64), 64)

    def both_cores(t, acc, got):
        return acc[rows_of(t, core), :] + got.astype(F32)

    other_core = yh * 2 + 1 - core
    other_chip = (1 - yh) * 2 + core
    for t in range(2):
        s.se1[t] = s.pe[rows_of(t, 1 - core), :].astype(BF)
    ce1 = remote(s.se1, s.re1, s.ce.at[0], s.ce.at[1], other_core, gy)
    ce1.start()

    weights = ((s.wqv, s.pq), (s.wgv, s.pg), (s.wuv, s.pu))
    loads[8].wait()

    def prepare(nrm, part, pieces):
        start, rows = parts[part]
        spots = []
        for ring_at, dy, dr in pieces:
            a = lax.rem(yl + dy, 2)
            r = lax.rem((x, z)[part] + 4 - dr, 4)
            spots.append((a, ring_at, r) if part == 0 else (a, r, ring_at))
        for i, (a, zz, xx) in enumerate(spots):
            block = s.xt0[zz, a, xx] if part == 0 else s.xt1[xx, a, zz]
            nrm[i * rows : (i + 1) * rows, :] = normalize(block, place(a, zz, xx) * COLS + start, rows)
        return nrm[0 : len(spots) * rows, :].T, spots

    def project(part, lhs, spots, only):
        start, rows = parts[part]
        for w, acc in only:
            rhs = [w[a, zz, xx, start : start + rows, :] for a, zz, xx in spots]
            acc[...] += dot(lhs, jnp.concatenate(rhs, axis=0))

    def chunk(group, carry):
        @pl.when(group > 0)
        def _():
            hand_on(group)

        dr = group + group // 2 - 2 * (group // 3)
        for part in range(2):
            near = [(along(part, d), dy, dr) for dy in range(2) for d in (0, 1, 3)]
            project(part, *prepare((s.nrm0, s.nrm1)[part], part, near), weights)

        return carry

    lax.fori_loop(0, 4, chunk, 0)
    ready = []
    for part in range(2):
        for group in range(4):
            arrived(part, 2, group)
        distant = [(along(part, 2), dy, dr) for dy in range(2) for dr in range(4)]
        ready.append((part, *prepare((s.nrm0, s.nrm1)[part], part, distant)))
        project(*ready[part], weights[:1])

    for t in range(2):
        s.sq1[t] = s.pq[rows_of(t, 1 - core), :].astype(BF)
    cq1 = remote(s.sq1, s.rq1, s.cq.at[0], s.cq.at[1], other_core, gy)
    cq1.start()
    ce1.wait_recv()
    for t in range(2):
        entries = both_cores(t, s.pe, s.re1[t])
        s.msg[t] = jnp.zeros((512, 128), F32)
        for k in range(4):
            s.ef[t, k] = entries[:, 128 * k : 128 * k + 128]
            for i in range(2):
                s.msg[t, pl.ds(6 + 4 * i + k, 32, stride=16), :] = s.ef[t, k, pl.ds(i, 32, stride=2), :]
    cq1.wait_recv()

    for t in range(2):
        query = both_cores(t, s.pq, s.rq1[t])
        for k in range(3):
            s.qf[t, k] = query[:, 128 * k : 128 * k + 128]
            for i in range(2):
                s.msg[t, pl.ds(3 * i + k, 32, stride=16), :] = s.qf[t, k, pl.ds(i, 32, stride=2), :]
    s.mq[...] = s.msg[...].astype(BF).reshape(64, 16, 128)
    own_slot = yh * 32 + gy
    partners = [(1 - yh, p) for p in others + [gy]] + [(yh, p) for p in others]
    for to, p in partners:
        remote(
            s.mq.at[to * 32 + p], s.mr.at[own_slot], s.mqs.at[0], s.mqs.at[1], to * 2 + core, p
        ).start()
    s.mr[own_slot] = s.mq[own_slot]

    for item in ready:
        project(*item, weights[1:])
    for t in range(2):
        give = rows_of(t, 1 - core)
        s.sg1[t, 0] = s.pg[give, :].astype(BF)
        s.sg1[t, 1] = s.pu[give, :].astype(BF)
    cg1 = remote(s.sg1, s.rg1, s.cg.at[0, 0], s.cg.at[1, 0], other_core, gy)
    cg1.start()
    cg1.wait_recv()
    s.sg2[0] = both_cores(1 - yh, s.pg, s.rg1[1 - yh, 0]).astype(BF)
    s.sg2[1] = both_cores(1 - yh, s.pu, s.rg1[1 - yh, 1]).astype(BF)
    cg2 = remote(s.sg2, s.rg2, s.cg.at[0, 1], s.cg.at[1, 1], other_chip, gy)
    cg2.start()

    first_row = (gx * 32 + gy) * 2
    turns = []
    for i in range(2):
        at = jnp.full((8, DH), lens[first_row + i].astype(F32), F32)
        turns.append([v[0:1] for v in rope_tables(at, 0, (8, DH))])

    many_q = s.mr.at[pl.ds(0, 63)]
    pltpu.make_async_copy(many_q, many_q, s.mqs.at[1]).wait()
    rest[1].wait()
    rest[2].wait()
    s.msg[...] = s.mr[...].reshape(2, 512, 128).astype(F32)
    s.msg[0] = s.msg[0] + s.msg[1]
    scale = 1.0 / math.sqrt(DH)
    s.aback[...] = jnp.zeros((32, 8, 128), F32)
    replies = []
    for i in range(2):
        for k in range(3):
            s.pieces[pl.ds(k, 32, stride=3), :] = s.msg[0, pl.ds(3 * i + k, 32, stride=16), :]
        q = jnp.concatenate(
            [s.pieces[pl.ds(0, 48, stride=2), :], s.pieces[pl.ds(1, 48, stride=2), :]], axis=1
        )
        cosine, sine = turns[i]
        q = q * cosine + swap_pairs(q) * sine
        qb = q.astype(BF)
        entry = [
            jnp.sum(s.msg[0, pl.ds(6 + 4 * i + k, 32, stride=16), :], axis=0, keepdims=True)
            for k in range(4)
        ]
        length = lens[first_row + i]
        key = jnp.broadcast_to(jnp.concatenate(entry[0:2], axis=1), (8, DH))
        value = jnp.concatenate(entry[2:4], axis=1).astype(BF).astype(F32)
        key = (key * cosine + swap_pairs(key) * sine)[0:1].astype(BF).astype(F32)
        scores = (
            lax.dot_general(qb, s.keys[i], (((1,), (1,)), ((), ())), preferred_element_type=F32) * scale
        )
        position = lax.broadcasted_iota(jnp.int32, (H, CTX), 1)
        scores = jnp.where(position < length, scores, -1e30)
        own = jnp.sum(qb.astype(F32) * key, axis=1, keepdims=True) * scale
        peak = jnp.maximum(jnp.max(scores, axis=1, keepdims=True), own)
        expd = jnp.exp(scores - peak)
        own_exp = jnp.exp(own - peak)
        denom = jnp.sum(expd, axis=1, keepdims=True) + own_exp
        weights = (expd / denom).astype(BF)
        own_weight = (own_exp / denom).astype(BF).astype(F32)
        mixed = dot(weights, s.vals[i]) + own_weight * value
        s.pieces[pl.ds(0, 48, stride=2), :] = mixed[:, 0:128]
        s.pieces[pl.ds(1, 48, stride=2), :] = mixed[:, 128:256]
        for k in range(3):
            replies.append((3 * i + k, s.pieces[pl.ds(k, 32, stride=3), :]))
    for row, piece in replies:
        s.msg[0, pl.ds(row, 32, stride=8), :] = piece
    s.aback[...] = s.msg[0, 0:256, :].reshape(32, 8, 128)

    for to, p in partners:
        remote(
            s.aback.at[p], s.abackr.at[own_slot], s.abs_.at[0], s.abs_.at[1], to * 2 + core, p
        ).start()
    s.abackr[own_slot] = s.aback[gy]

    cg2.wait_recv()
    gate = both_cores(yh, s.pg, s.rg1[yh, 0]) + s.rg2[0].astype(F32)
    up = both_cores(yh, s.pu, s.rg1[yh, 1]) + s.rg2[1].astype(F32)
    s.hidall[gx] = (gate / (1.0 + jnp.exp(-gate)) * up).astype(BF)
    gather_hidden = [
        remote(
            s.hidall.at[gx], s.hidall.at[gx], s.gh.at[0, d - 1], s.gh.at[1, d - 1], lax.rem(gx + d, 4), gy
        )
        for d in range(1, 4)
    ]
    for cp in gather_hidden:
        cp.start()


    for cp in gather_hidden:
        cp.wait_recv()
    rest[3].wait()

    def pair_of(half):
        return lax.rem(z // 2 + 1 + half, 2)

    def down(cols):
        return dot(s.hidall[...].reshape(ROWS, FC), s.wdv[:, cols])

    def columns_of(a, half):
        return pl.ds(pl.multiple_of((2 * a + pair_of(half)) * WIDE, 128), WIDE)

    def early_down(a, carry):
        s.outp[a] = down(columns_of(a, 0))
        return carry

    many_a = s.abackr.at[pl.ds(0, 63)]
    pltpu.make_async_copy(many_a, many_a, s.abs_.at[1]).wait()
    s.msg[0] = s.abackr[...].reshape(512, 128)
    gather_att = []
    for t in range(2):
        at = 2 * t + core
        for k in range(3):
            for i in range(2):
                s.att64[t, k, pl.ds(i, 32, stride=2), :] = s.msg[
                    0, pl.ds(256 * t + 3 * i + k, 32, stride=8), :
                ]
            s.attall[at, :, 128 * k : 128 * k + 128] = s.att64[t, k].astype(BF)
        gather_att.append(
            remote(s.attall.at[at], s.attall.at[at], s.ga.at[0, t], s.ga.at[1, t], other_core, gy)
        )
        gather_att[t].start()
    rest[4].wait()
    for cp in gather_att:
        cp.wait_recv()

    outs = ((s.e0, s.r0, s.y0, s.c0, s.s0), (s.e1, s.r1, s.y1, s.c1, s.s1))

    def block(part, ring_at, dy, dr):
        a = lax.rem(yl + dy, 2)
        r = lax.rem((x, z)[part] + dr, 4)
        start, rows = parts[part]
        where = (a, ring_at, r) if part == 0 else (a, r, ring_at)
        return s.eT.at[(*where, pl.ds(start, rows))]

    def turned_out(half):
        def one(a, carry):
            cols = columns_of(a, half)
            v = down(cols)
            v = v + dot(s.attall[...].reshape(ROWS, QC), s.wov[:, cols])
            s.eT[a, pl.ds(pair_of(half) * 2, 2)] = v.T.astype(BF).reshape(2, 4, COLS, ROWS)
            return carry

        lax.fori_loop(0, 2, one, 0)

    legs = []

    def leg(part, kind, dy, dr, src, dst, j):
        sem = outs[part][0]
        cp = remote(src, dst, sem.at[0, kind, dy, dr], sem.at[1, kind, dy, dr], gx, ring[1 - part](j))
        cp.start()
        legs.append(cp)
        return cp

    steps = (1, 3)
    ways = (2, 1, 3, 0)
    early = {}

    def send_early(part):
        for dr in ways:
            for dy in range(2):
                early[part, dy, dr] = leg(
                    part, 0, dy, dr, block(part, along(part, 2), dy, dr), outs[part][2].at[dy, dr], steps[dy]
                )

    turned_out(0)
    send_early(0)
    turned_out(1)
    send_early(1)
    plain, joined = {}, {}
    for dr in ways:
        for part in range(2):
            for dy in range(2):
                way = 1 - dy
                plain[part, dy, dr] = leg(
                    part, 1, dy, dr,
                    block(part, along(part, steps[way]), dy, dr), outs[part][1].at[way, dy, dr], steps[way],
                )
    for dr in ways:
        for part in range(2):
            _, got, relay, both, _ = outs[part]
            for dy in range(2):
                early[part, dy, dr].wait_recv()
                mine = block(part, along(part, steps[dy]), dy, dr)
                both[dy, dr] = (mine[...].astype(F32) + relay[dy, dr].astype(F32)).astype(BF)
                joined[part, dy, dr] = leg(
                    part, 2, dy, dr, both.at[dy, dr], got.at[dy, dy, dr], steps[dy]
                )

    last0 = {
        k: remote(s.s0.at[k], s.r0b.at[k], s.f0.at[0, k], s.f0.at[1, k], gx, plane[0](k))
        for k in range(1, 8)
    }
    last1 = {
        k: remote(s.s1.at[k], s.r1b.at[k], s.f1.at[0, k], s.f1.at[1, k], gx, plane[1](k))
        for k in range(1, 8)
    }

    def summed(part, dy, dr):
        plain[part, dy, dr].wait_recv()
        joined[part, dy, dr].wait_recv()
        got = outs[part][1]
        v = block(part, along(part, 0), dy, dr)[...].astype(F32)
        return v + got[0, dy, dr].astype(F32) + got[1, dy, dr].astype(F32)

    order = [4 * dy + dr for dr in ways for dy in (1, 0)][:-1]
    for k in order:
        for part in range(2):
            outs[part][4][k] = summed(part, k // 4, k % 4).astype(BF)
            (last0, last1)[part][k].start()
    v0 = tok[0:PA, :].astype(F32) + summed(0, 0, 0)
    v1 = tok[PA:COLS, :].astype(F32) + summed(1, 0, 0)
    for k in order:
        last0[k].wait_recv()
        v0 = v0 + s.r0b[k].astype(F32)
    out[0:PA, :] = v0
    for k in order:
        last1[k].wait_recv()
        v1 = v1 + s.r1b[k].astype(F32)
    out[PA:COLS, :] = v1

    for group in (
        stat_z, stat_plane, stat_gx, (ce1, cq1, cg1, cg2),
        gather_hidden, gather_att, first0.values(), first1.values(), last0.values(), last1.values(),
    ):
        for cp in group:
            cp.wait_send()
    for cp in legs:
        cp.wait_send()
    for part in range(2):
        two = xts[part].at[0, 0, pl.ds(0, 2)]
        for j in range(1, 4):
            for group in range(4):
                pltpu.make_async_copy(two, two, bs[part].at[0, j, group]).wait()
    pltpu.make_async_copy(many_q, many_q, s.mqs.at[0]).wait()
    pltpu.make_async_copy(many_a, many_a, s.abs_.at[0]).wait()


def body(
    tokens, ln_gain, w_query, w_entries, w_out, w_gate, w_up, w_down, cache_keys, cache_values, lengths
):
    vmem = pl.BlockSpec(memory_space=pltpu.VMEM)
    hbm = pl.BlockSpec(memory_space=pl.ANY)
    return pl.pallas_call(
        kernel,
        out_shape=jax.ShapeDtypeStruct((COLS, ROWS), F32),
        in_specs=[vmem, vmem, pl.BlockSpec(memory_space=pltpu.SMEM)] + [hbm] * 8,
        out_specs=vmem,
        scratch_shapes=[pltpu.VMEM(shape, kind) for shape, kind in SCRATCH.values()]
        + [pltpu.SemaphoreType.DMA(shape) for shape in SEMS.values()],
        compiler_params=pltpu.CompilerParams(
            collective_id=0, has_side_effects=True, vmem_limit_bytes=60 << 20
        ),
        name="layer",
    )(
        tokens.T,
        ln_gain.reshape(36, 128),
        lengths,
        w_query.reshape(2, 4, 4, COLS, QC),
        w_gate.T,
        w_up.T,
        w_entries,
        w_out,
        w_down,
        cache_keys,
        cache_values,
    ).T


def solution(mesh):
    return jax.shard_map(
        body,
        mesh=mesh,
        in_specs=(
            P(None, ("gx", "gy")),
            P("gx"),
            P("gx", "gy"),
            P(("gx", "gy"), None),
            P("gy", "gx"),
            P("gx", "gy"),
            P("gx", "gy"),
            P("gy", "gx"),
            P(("gx", "gy"), None, None),
            P(("gx", "gy"), None, None),
            P(None),
        ),
        out_specs=P(None, ("gx", "gy")),
        check_vma=False,
    )
```
